256 devices in a mesh: tile: 32 (over x, z), band: 8 (over y, core).
Axes of the slice: x: 4, y: 4, z: 8, core: 2. Of those that a mesh axis runs over, the one named last changes fastest.
Arguments:
- traces: bfloat16 [65536, 1024], P('tile', 'band'), may hold values from -6 to 6
- route: int32 [65536, 1], P('tile'), may hold values from 0 to 31; in each aligned block of 2048 rows (0 to 2047, 2048 to 4095, ...) at most 128 rows name the same one
- mid_x: int32 [65536], P('tile'), may hold values from 0 to 255
- mid_y: int32 [65536], P('tile'), may hold values from 0 to 255
- band_low: int32 [32], P('tile'), may hold values from 0 to 7
- band_high: int32 [32], P('tile'), may hold values from 25 to 32
- offset_bin: int32 [32], P('tile'), may hold values from 0 to 7
- azimuth_bin: int32 [32], P('tile'), may hold values from 0 to 11
Outputs:
- amo_out: float32 [32, 32, 256, 512], P('tile', 'band')
The draws below stay inside these ranges and needn't reach their ends.
Inputs may be any that keep to these rules, and one draw needn't show every extreme that they name: `route`: within each aligned block of 2048 traces (one shot shard) no tile is named more than 128 times, a bound that some block reaches.
All inputs are finite; a program needn't handle non-finite values.
Results may differ from the reference program's by a relative error of at most 0.009.
Values may be sent and summed in bfloat16 or wider, within the bound.
No kernel may reach another device: no remote copies, remote signals or barrier semaphores. Data moves between devices by JAX's collectives and lax.ppermute only.
A program may use at most 64 MiB of HBM per device.

```python
import math
import jax
import jax.numpy as jnp
import numpy as np
from jax import lax

NT = 1024
MIDS = 256
OFFSETS = 8
AZIMUTHS = 12
TR_DEV = 2048
TILES = 32
TRACES = 65536
NF = 32
CAP = 128
N_TILE = 32


def place_ends(values, stream_key, least, top_value):
    longest = values.shape.index(max(values.shape))
    spots = []
    for shift in (0, 1):
        where = [jax.random.randint(jax.random.fold_in(stream_key, axis), (), 0, length) for axis, length in enumerate(values.shape)]
        where[longest] = (where[longest] + shift) % values.shape[longest]
        spots.append(tuple(where))
    return values.at[spots[0]].set(least).at[spots[1]].set(top_value)


def levels(rng, dims, shards, least, high):
    def one(dim, shards_of):
        heights = jax.random.uniform(jax.random.fold_in(jax.random.fold_in(rng, 6), dim), (shards_of,), jnp.float32, least / len(shards), high / len(shards))
        return jnp.repeat(jnp.exp(heights), dims[dim] // shards_of).reshape((-1,) + (1,) * (len(dims) - dim - 1))

    factor_of = one(*shards[0])
    for cut in shards[1:]:
        factor_of = factor_of * one(*cut)
    return factor_of


def shared_out(own_key, own, number, rows, number_of, top, limit, skew):
    sequence = jax.random.permutation(own_key, number_of)
    crowded, usual = shares(number_of, rows * top, limit, skew, True), shares(number_of, rows * top, limit, skew, False)
    places = jnp.arange(number_of)

    def named(lengths, turn):
        used = int((lengths > 0).sum())
        fixed = max(1, used // 4)
        shifted = fixed + (places - fixed + turn * (used - fixed)) % max(1, number_of - fixed)
        return jnp.zeros((number_of,), jnp.int32).at[sequence[jnp.where(places < fixed, places, shifted)]].set(jnp.asarray(lengths, jnp.int32))

    lengths = jnp.where(number % 4 == 0, named(crowded, number // 4), named(usual, number - number // 4 - 1))
    mixed = jax.random.permutation(jax.random.fold_in(own, 3), number_of)
    donor, receiver = mixed[0:number_of // 2 * 2:2], mixed[1:number_of // 2 * 2:2]
    slack = jnp.minimum(lengths[donor] - 1, limit - lengths[receiver]) // 2
    slack = jnp.where((donor == sequence[0]) | (receiver == sequence[0]) | (lengths[receiver] == 0), 0, jnp.maximum(slack, 0))
    shifted = jax.random.randint(jax.random.fold_in(own, 4), (number_of // 2,), 0, 1 << 20) % (slack + 1)
    lengths = lengths.at[donor].add(-shifted).at[receiver].add(shifted)
    items = jnp.searchsorted(jnp.cumsum(lengths), jnp.arange(rows * top), side="right").astype(jnp.int32)
    listing = items.reshape(top, rows).T
    listing = listing[jax.random.permutation(jax.random.fold_in(own, 1), rows)]
    turn = jax.random.randint(jax.random.fold_in(own, 2), (rows, 1), 0, top)
    return jnp.take_along_axis(listing, (jnp.arange(top)[None, :] + turn) % top, axis=1)


def shares(amount, total, bound, lean, full):
    weights = [(1 << 20) // math.isqrt(standing ** lean) + 1 for standing in range(1, amount + 1)]
    largest = bound if full else min(bound, max(-(-total // amount), total * weights[0] // sum(weights)))
    least = 1 if total - largest >= amount - 1 else 0
    given, surplus = [largest] + [least] * (amount - 1), total - largest - least * (amount - 1)
    while surplus > 0:
        candidates = [i for i in range(1, amount) if given[i] < largest] or [i for i in range(1, amount) if given[i] < bound]
        pool, remaining = sum([weights[i] for i in candidates]), surplus
        for i in candidates:
            extra = min(bound - given[i], max(1, remaining * weights[i] // pool), surplus)
            given[i] = given[i] + extra
            surplus = surplus - extra
    return np.array(given)


def scatter_about(key, dims, scale, limit, shards=(), kind=jnp.bfloat16):
    loudness = levels(key, dims, shards, -0.22, 0.18) if shards else 1.0
    result = jax.random.normal(key, dims, jnp.float32) * scale * loudness
    return jnp.minimum(jnp.maximum(result, -limit), limit).astype(kind)


def setup_inputs(seed: int = 0) -> dict:
    keys = jax.random.split(jax.random.key(seed), 9)
    traces = scatter_about(keys[0], (TRACES, NT), 1.0, 6.0, ((0, 32), (1, 8)))
    route_keys = jax.random.split(jax.random.fold_in(keys[1], 1), TRACES // TR_DEV)
    route_turns = jax.random.permutation(jax.random.fold_in(keys[1], 3), TRACES // TR_DEV)
    route = jax.vmap(lambda own, number: shared_out(jax.random.fold_in(keys[1], 2), own, number, TR_DEV, TILES, 1, CAP, 2))(route_keys, route_turns).reshape((TRACES, 1))
    mid_x = place_ends(jax.random.randint(keys[2], (TRACES,), 0, MIDS), jax.random.fold_in(keys[2], 1), 0, MIDS - 1).astype(jnp.int32)
    mid_y = place_ends(jax.random.randint(keys[3], (TRACES,), 0, MIDS), jax.random.fold_in(keys[3], 1), 0, MIDS - 1).astype(jnp.int32)
    band_low = place_ends(jax.random.randint(keys[4], (TILES,), 0, NF // 4), jax.random.fold_in(keys[4], 1), 0, (NF // 4) - 1).astype(jnp.int32)
    band_high = place_ends(jax.random.randint(keys[5], (TILES,), 3 * NF // 4 + 1, NF + 1), jax.random.fold_in(keys[5], 1), 3 * NF // 4 + 1, NF).astype(jnp.int32)
    offset_bin = place_ends(jax.random.randint(keys[6], (TILES,), 0, OFFSETS), jax.random.fold_in(keys[6], 1), 0, OFFSETS - 1).astype(jnp.int32)
    azimuth_bin = place_ends(jax.random.randint(keys[7], (TILES,), 0, AZIMUTHS), jax.random.fold_in(keys[7], 1), 0, AZIMUTHS - 1).astype(jnp.int32)
    return {"traces": traces, "route": route, "mid_x": mid_x, "mid_y": mid_y, "band_low": band_low, "band_high": band_high, "offset_bin": offset_bin, "azimuth_bin": azimuth_bin}


LOG_ANCHOR = 64.0


def log_omegas(first_index, freq_count, trace_length):
    log_span = math.log((trace_length + LOG_ANCHOR) / LOG_ANCHOR)
    steps_up = jnp.arange(freq_count, dtype=jnp.int32) + first_index + 1
    return steps_up.astype(jnp.float32) * (2.0 * math.pi / log_span)


def time_kernel(first_index, sample_count, trace_length, freq_count):
    samples = (jnp.arange(sample_count, dtype=jnp.int32) + first_index).astype(jnp.float32)
    stretch = jnp.log((samples + LOG_ANCHOR) / LOG_ANCHOR)
    omegas = log_omegas(0, freq_count, trace_length)
    angles = stretch[:, None] * omegas[None, :]
    weight = trace_length ** -0.5
    stacked = jnp.stack([jnp.cos(angles) * weight, -jnp.sin(angles) * weight], axis=2)
    return stacked.reshape(sample_count, 2 * freq_count).astype(jnp.bfloat16)


def forward_rows(positions, grid_size):
    wave_index = jnp.arange(grid_size, dtype=jnp.int32)
    phase_turns = (positions[:, None] * wave_index[None, :]) % grid_size
    angles = phase_turns.astype(jnp.float32) * (2.0 * math.pi / grid_size)
    return jnp.cos(angles), -jnp.sin(angles)


def inverse_blocks(grid_size):
    wave_index = jnp.arange(grid_size, dtype=jnp.int32)
    phase_turns = (wave_index[:, None] * wave_index[None, :]) % grid_size
    angles = phase_turns.astype(jnp.float32) * (2.0 * math.pi / grid_size)
    cosine_table = jnp.cos(angles)
    sine_table = jnp.sin(angles)
    left_side = jnp.concatenate([jnp.concatenate([cosine_table, -sine_table], axis=1),
                                 jnp.concatenate([sine_table, cosine_table], axis=1)], axis=0)
    right_side = jnp.concatenate([jnp.concatenate([cosine_table, sine_table], axis=1),
                                  jnp.concatenate([-sine_table, cosine_table], axis=1)], axis=0)
    return left_side.astype(jnp.bfloat16), right_side.astype(jnp.bfloat16)


def accumulate(spectra, pos_x, pos_y, grid_size, weight):
    row_total = spectra.shape[0]
    freq_count = spectra.shape[1] // 2
    row_block = math.gcd(row_total, 512)

    def add_rows(step_number, running):
        start_row = step_number * row_block
        spectra_rows = lax.dynamic_slice_in_dim(spectra, start_row, row_block, 0)
        spectra_rows = spectra_rows.astype(jnp.float32).reshape(row_block, freq_count, 2)
        block_x = lax.dynamic_slice_in_dim(pos_x, start_row, row_block, 0)
        block_y = lax.dynamic_slice_in_dim(pos_y, start_row, row_block, 0)
        cosine_x, sine_x = forward_rows(block_x, grid_size)
        cosine_y, sine_y = forward_rows(block_y, grid_size)
        real_part = spectra_rows[:, :, 0:1] * weight
        imag_part = spectra_rows[:, :, 1:2] * weight
        left_real = real_part * cosine_x[:, None, :] - imag_part * sine_x[:, None, :]
        left_imag = real_part * sine_x[:, None, :] + imag_part * cosine_x[:, None, :]
        left_rows = jnp.concatenate([left_real, left_imag], axis=2).astype(jnp.bfloat16)
        left_rows = left_rows.reshape(row_block, freq_count * 2 * grid_size)
        right_rows = jnp.concatenate([cosine_y, sine_y], axis=1).astype(jnp.bfloat16)
        return running + lax.dot_general(left_rows, right_rows, (((0,), (0,)), ((), ())),
                                         preferred_element_type=jnp.float32)

    running = jnp.zeros((freq_count * 2 * grid_size, 2 * grid_size), jnp.float32)
    running = lax.fori_loop(0, row_total // row_block, add_rows, running)
    running = running.reshape(freq_count, 2, grid_size, 2, grid_size)
    real_part = running[:, 0, :, 0, :] - running[:, 1, :, 1, :]
    imag_part = running[:, 0, :, 1, :] + running[:, 1, :, 0, :]
    return real_part, imag_part


def amo_phase(omegas, offset_value, azimuth_value, grid_size):
    wave_index = jnp.arange(grid_size, dtype=jnp.int32)
    signed = jnp.where(wave_index >= grid_size // 2, wave_index - grid_size, wave_index)
    wavenumber = signed.astype(jnp.float32) * (2.0 * math.pi / grid_size)
    offset_length = (offset_value.astype(jnp.float32) + 1.0) * 0.5
    azimuth_angle = azimuth_value.astype(jnp.float32) * (math.pi / AZIMUTHS)
    inline = wavenumber[:, None] * (offset_length * jnp.cos(azimuth_angle)) + \
        wavenumber[None, :] * (offset_length * jnp.sin(azimuth_angle))
    along_target = wavenumber[:, None] * offset_length + jnp.zeros((1, grid_size), jnp.float32)
    change = jnp.log1p(along_target * along_target) - jnp.log1p(inline * inline)
    return 0.5 * omegas[:, None, None] * change[None, :, :]


def finish(real_part, imag_part, phase_table, live_mask, grid_size):
    cosine_phase = jnp.cos(phase_table)
    sine_phase = jnp.sin(phase_table)
    moved_real = (real_part * cosine_phase - imag_part * sine_phase) * live_mask[:, None, None]
    moved_imag = (real_part * sine_phase + imag_part * cosine_phase) * live_mask[:, None, None]
    stacked = jnp.concatenate([moved_real, moved_imag], axis=1).astype(jnp.bfloat16)
    left_side, right_side = inverse_blocks(grid_size)
    halfway = jnp.einsum("ab,fbc->fac", left_side.astype(jnp.float32), stacked.astype(jnp.float32))
    halfway = halfway.astype(jnp.bfloat16)
    across = jnp.concatenate([halfway[:, :grid_size, :], halfway[:, grid_size:, :]], axis=2)
    regular_image = jnp.einsum("fab,bc->fac", across.astype(jnp.float32), right_side.astype(jnp.float32))
    return regular_image * (1.0 / grid_size)


def reference(traces, route, mid_x, mid_y, band_low, band_high, offset_bin, azimuth_bin):
    capacity = 2 * TR_DEV // N_TILE
    receive = N_TILE * capacity
    kernel = time_kernel(0, NT, NT, NF)
    spectra = jnp.dot(traces, kernel, preferred_element_type=jnp.float32).astype(jnp.bfloat16)
    target = route[:, 0]
    one_hot = (target.reshape(N_TILE, TR_DEV)[:, :, None] ==
               jnp.arange(N_TILE, dtype=jnp.int32)[None, None, :]).astype(jnp.int32)
    earlier = jnp.cumsum(one_hot, axis=1) - one_hot
    within = jnp.sum(earlier * one_hot, axis=2).reshape(TRACES)
    source_shard = jnp.arange(TRACES, dtype=jnp.int32) // TR_DEV
    slot_index = source_shard * capacity + within
    owner_table = jnp.full((N_TILE, receive), TRACES, jnp.int32)
    owner_table = owner_table.at[target, slot_index].set(jnp.arange(TRACES, dtype=jnp.int32))
    spectra_pad = jnp.concatenate([spectra, jnp.zeros((1, 2 * NF), jnp.bfloat16)], axis=0)
    x_pad = jnp.concatenate([mid_x, jnp.zeros((1,), jnp.int32)])
    y_pad = jnp.concatenate([mid_y, jnp.zeros((1,), jnp.int32)])
    omegas = log_omegas(0, NF, NT)
    frequencies = jnp.arange(NF, dtype=jnp.int32)

    def one_tile(tile_number):
        slot_rows = owner_table[tile_number]
        real_part, imag_part = accumulate(spectra_pad[slot_rows], x_pad[slot_rows], y_pad[slot_rows],
                                          MIDS, TR_DEV ** -0.5)
        live_mask = ((frequencies >= band_low[tile_number]) &
                     (frequencies < band_high[tile_number])).astype(jnp.float32)
        phase_table = amo_phase(omegas, offset_bin[tile_number], azimuth_bin[tile_number], MIDS)
        return finish(real_part, imag_part, phase_table, live_mask, MIDS)

    return lax.map(one_tile, jnp.arange(N_TILE, dtype=jnp.int32))
```

```python
import math

import jax
import jax.numpy as jnp
import numpy as np
from jax import lax
from jax.experimental import pallas as pl
from jax.experimental.pallas import tpu as pltpu
from jax.sharding import PartitionSpec as P

MIDS = 256
HALF = 128
AZIMUTHS = 12
F_DEV = 4
COLS = 2 * F_DEV
BANDS = 8
TILES = 32
ROWS = 2048
SAMPLES = 128
NT = 1024
CAP = 128
ANCHOR = 64.0
LOG_SPAN = math.log((NT + ANCHOR) / ANCHOR)
CHUNK = 4
NT_DIMS = (((1,), (1,)), ((), ()))
VMEM_BYTES = 56 * 1024 * 1024


def time_kernel_blocks():
    stretch = np.log((np.arange(NT) + ANCHOR) / ANCHOR)
    omegas = (np.arange(F_DEV * BANDS) + 1) * (2.0 * math.pi / LOG_SPAN)
    angles = omegas[:, None] * stretch[None, :]
    stacked = np.stack([np.cos(angles), -np.sin(angles)], axis=1) * NT**-0.5
    stacked = stacked.reshape(COLS * BANDS, BANDS, SAMPLES).transpose(1, 0, 2)
    return stacked.astype(np.float32).astype(jnp.bfloat16)


def folded_table():
    turns = (np.arange(MIDS)[:, None] * np.arange(HALF)[None, :]) % MIDS
    angles = turns * (2.0 * math.pi / MIDS)
    sines = np.sin(angles)
    sines[:, 0] = (-1.0) ** np.arange(MIDS)
    table = np.concatenate([np.cos(angles), sines], axis=1)
    return table.astype(np.float32).astype(jnp.bfloat16)


def sincos_turns(turns):
    quarters = (turns - jnp.round(turns)) * 4.0
    quadrant = jnp.round(quarters)
    angle = (quarters - quadrant) * (math.pi / 2)
    square = angle * angle
    sine = angle * (1.0 + square * (-1.0 / 6 + square * (1.0 / 120 + square * (-1.0 / 5040))))
    cosine = 1.0 + square * (
        -0.5 + square * (1.0 / 24 + square * (-1.0 / 720 + square * (1.0 / 40320)))
    )
    index = quadrant.astype(jnp.int32)
    odd = (index & 1) == 1
    low, high = jnp.where(odd, sine, cosine), jnp.where(odd, cosine, sine)
    cos_out = jnp.where(((index + 1) & 2) == 2, -low, low)
    sin_out = jnp.where((index & 2) == 2, -high, high)
    return cos_out, sin_out


def partial_kernel(kern_hbm, traces_hbm, out_ref, kern, rows, sems):
    band = lax.axis_index("band")
    get_kern = pltpu.make_async_copy(kern_hbm.at[band], kern, sems.at[0])
    get_rows = pltpu.make_async_copy(traces_hbm, rows, sems.at[1])
    get_kern.start()
    get_rows.start()
    get_kern.wait()
    get_rows.wait()
    part = lax.dot_general(kern[...], rows[...], NT_DIMS, preferred_element_type=jnp.float32)
    half = ROWS // 2
    for b in range(BANDS):
        block = part[b * COLS : (b + 1) * COLS]
        out_ref[b] = jnp.concatenate([block[:, :half], block[:, half:]], axis=0).astype(
            jnp.bfloat16
        )


def signed_folded(shape, dim):
    index = lax.broadcasted_iota(jnp.int32, shape, dim)
    signed = jnp.where(index < HALF, index, jnp.where(index == HALF, -HALF, HALF - index))
    return signed.astype(jnp.float32) * (2.0 * math.pi / MIDS)


def tables_kernel(
    route_ref, low_ref, high_ref, offset_ref, azimuth_ref, trig_ref, slot_ref, phase_ref
):
    block = MIDS
    row_i = lax.broadcasted_iota(jnp.int32, (block, block), 0)
    col_i = lax.broadcasted_iota(jnp.int32, (block, block), 1)
    upper = jnp.where(row_i < col_i, 1.0, 0.0).astype(jnp.bfloat16)
    tile_i = lax.broadcasted_iota(jnp.int32, (TILES, block), 0)
    slot_i = lax.broadcasted_iota(jnp.int32, (CAP, block), 0)
    carry = jnp.zeros((TILES, 1), jnp.float32)
    for step in range(ROWS // block):
        cut = slice(step * block, (step + 1) * block)
        member = jnp.where(tile_i == route_ref[:, cut], 1.0, 0.0)
        earlier = jnp.dot(
            member.astype(jnp.bfloat16), upper, preferred_element_type=jnp.float32
        )
        rank = jnp.sum(member * (earlier + carry), axis=0, keepdims=True).astype(jnp.int32)
        slot_ref[:, cut] = jnp.where(slot_i == rank, 1.0, 0.0).astype(jnp.bfloat16)
        carry = carry + jnp.sum(member, axis=1, keepdims=True)
    band = lax.axis_index("band")
    first = band * F_DEV
    h = (offset_ref[0].astype(jnp.float32) + 1.0) * 0.5
    kx = signed_folded((MIDS, MIDS), 0)
    ky = signed_folded((MIDS, MIDS), 1)
    inline = kx * (h * trig_ref[0]) + ky * (h * trig_ref[1])
    along = kx * h
    change = jnp.log1p(along * along) - jnp.log1p(inline * inline)
    unit = change * (0.5 / LOG_SPAN)
    turn_c, turn_s = sincos_turns(unit)
    cos_f, sin_f = sincos_turns(unit * (first + 1).astype(jnp.float32))
    scale = ROWS**-0.5 / MIDS
    for f in range(F_DEV):
        live = (first + f >= low_ref[0]) & (first + f < high_ref[0])
        weight = jnp.where(live, scale, 0.0)
        phase_ref[0, f] = cos_f * weight
        phase_ref[1, f] = sin_f * weight
        if f + 1 < F_DEV:
            cos_f, sin_f = cos_f * turn_c - sin_f * turn_s, cos_f * turn_s + sin_f * turn_c


def place_kernel(part_ref, slot_ref, route_ref, x_ref, y_ref, out_ref, masked):
    total = part_ref[0].astype(jnp.float32)
    for b in range(1, BANDS):
        total = total + part_ref[b].astype(jnp.float32)
    total = total.astype(jnp.bfloat16).astype(jnp.float32)
    spectra = jnp.concatenate([total[:COLS], total[COLS:]], axis=1)
    row = lax.broadcasted_iota(jnp.int32, (8, ROWS), 0)
    mids = jnp.where(
        row == 0, x_ref[...].astype(jnp.float32), jnp.where(row == 1, y_ref[...].astype(jnp.float32), 0.0)
    )
    values = jnp.concatenate([spectra, mids], axis=0)
    tile = jnp.broadcast_to(route_ref[...], (16, ROWS))
    for g in range(TILES):
        masked[g * 16 : (g + 1) * 16, :] = jnp.where(tile == g, values, 0.0).astype(jnp.bfloat16)
    placed = lax.dot_general(
        masked[...], slot_ref[...], NT_DIMS, preferred_element_type=jnp.float32
    )
    out_ref[...] = placed.astype(jnp.bfloat16).reshape(TILES, 16, CAP)


def tile_kernel(
    got_ref,
    table_hbm,
    tablet_hbm,
    phase_hbm,
    out_hbm,
    xa,
    xb,
    ya,
    yb,
    acc,
    table,
    tablet,
    phase,
    image,
    sems,
):
    copies = [
        pltpu.make_async_copy(table_hbm, table, sems.at[0]),
        pltpu.make_async_copy(tablet_hbm, tablet, sems.at[1]),
        pltpu.make_async_copy(phase_hbm, phase, sems.at[2]),
    ]
    for copy in copies:
        copy.start()
    iota = lax.broadcasted_iota(jnp.int32, (16, CAP), 0).astype(jnp.float32)
    one = jnp.ones((16, CAP), jnp.bfloat16)
    zero = jnp.zeros((16, CAP), jnp.bfloat16)

    def build(x_buf, y_buf, step):
        for i in range(CHUNK):
            part = got_ref[step * CHUNK + i].astype(jnp.float32)
            rows = [
                jnp.broadcast_to(part[c : c + 1], (16, CAP)).astype(jnp.bfloat16)
                for c in range(COLS + 2)
            ]
            cut = slice(i * CAP, (i + 1) * CAP)
            for r in range(MIDS // 16):
                here = (iota + (16.0 * r)).astype(jnp.bfloat16)
                in_x = here == rows[COLS]
                for c in range(COLS):
                    at = c * MIDS + r * 16
                    x_buf[at : at + 16, cut] = jnp.where(in_x, rows[c], zero)
                y_buf[r * 16 : (r + 1) * 16, cut] = jnp.where(here == rows[COLS + 1], one, zero)

    def add(x_buf, y_buf):
        acc[...] += lax.dot_general(
            x_buf[...], y_buf[...], NT_DIMS, preferred_element_type=jnp.float32
        )

    acc[...] = jnp.zeros_like(acc)
    steps = TILES // CHUNK
    build(xa, ya, 0)

    def pair(p, _):
        build(xb, yb, 2 * p + 1)
        add(xa, ya)
        build(xa, ya, jnp.minimum(2 * p + 2, steps - 1))
        add(xb, yb)
        return 0

    lax.fori_loop(0, steps // 2, pair, 0)
    for copy in copies:
        copy.wait()

    lane0 = lax.broadcasted_iota(jnp.int32, (MIDS, HALF), 1) == 0
    row0 = lax.broadcasted_iota(jnp.int32, (HALF, MIDS), 0) == 0
    bf = lambda v: v.astype(jnp.bfloat16)
    dot = lambda a, b: jnp.dot(a, b, preferred_element_type=jnp.float32)
    puts = []
    for f in range(F_DEV):
        u = dot(bf(acc[f * 512 : (f + 1) * 512]), table[...])
        cr, sr, ci, si = u[:MIDS, :HALF], u[:MIDS, HALF:], u[MIDS:, :HALF], u[MIDS:, HALF:]
        sr0, si0 = jnp.where(lane0, 0.0, sr), jnp.where(lane0, 0.0, si)
        h_r = [cr + si0, jnp.where(lane0, sr, cr - si)]
        h_i = [ci - sr0, jnp.where(lane0, si, ci + sr)]
        h = bf(jnp.concatenate(h_r + h_i, axis=1))
        v = dot(tablet[...], h)
        cr, sr, ci, si = v[:HALF, :MIDS], v[HALF:, :MIDS], v[:HALF, MIDS:], v[HALF:, MIDS:]
        sr0, si0 = jnp.where(row0, 0.0, sr), jnp.where(row0, 0.0, si)
        wpr, wpi = cr + si0, ci - sr0
        wmr, wmi = jnp.where(row0, sr, cr - si), jnp.where(row0, si, ci + sr)
        pc, ps = phase[0, f, :HALF], phase[1, f, :HALF]
        mc, ms = phase[0, f, HALF:], phase[1, f, HALF:]
        mpr, mpi = wpr * pc - wpi * ps, wpr * ps + wpi * pc
        mmr, mmi = wmr * mc - wmi * ms, wmr * ms + wmi * mc
        a_r = mpr + jnp.where(row0, 0.0, mmr)
        a_i = mpi + jnp.where(row0, 0.0, mmi)
        d_r = jnp.where(row0, mmr, mmi - mpi)
        d_i = jnp.where(row0, mmi, mpr - mmr)
        folded = jnp.concatenate(
            [jnp.concatenate([a_r, a_i], axis=1), jnp.concatenate([d_r, d_i], axis=1)], axis=0
        )
        q = dot(table[...], bf(folded))
        qpr, qmr, qpi, qmi = q[:, :HALF], q[:, HALF:MIDS], q[:, MIDS : MIDS + HALF], q[:, MIDS + HALF :]
        a_r = qpr + jnp.where(lane0, 0.0, qmr)
        a_i = qpi + jnp.where(lane0, 0.0, qmi)
        d_r = jnp.where(lane0, qmr, qmi - qpi)
        d_i = jnp.where(lane0, qmi, qpr - qmr)
        folded = jnp.concatenate(
            [jnp.concatenate([a_r, d_r], axis=1), jnp.concatenate([a_i, d_i], axis=1)], axis=0
        )
        w = dot(bf(folded), tablet[...])
        image[f, :, :MIDS] = w[:MIDS]
        image[f, :, MIDS:] = w[MIDS:]
        put = pltpu.make_async_copy(image.at[f], out_hbm.at[f], sems.at[3 + f])
        put.start()
        puts.append(put)
    for put in puts:
        put.wait()


VM = pl.BlockSpec(memory_space=pltpu.VMEM)
SM = pl.BlockSpec(memory_space=pltpu.SMEM)
ANY = pl.BlockSpec(memory_space=pl.ANY)
PARAMS = pltpu.CompilerParams(vmem_limit_bytes=VMEM_BYTES)


def cost(flops, moved):
    return pl.CostEstimate(flops=flops, bytes_accessed=moved, transcendentals=0)


def partial_spectra(kern, traces):
    return pl.pallas_call(
        partial_kernel,
        out_shape=jax.ShapeDtypeStruct((BANDS, 16, ROWS // 2), jnp.bfloat16),
        in_specs=[ANY, ANY],
        out_specs=VM,
        scratch_shapes=[
            pltpu.VMEM((COLS * BANDS, SAMPLES), jnp.bfloat16),
            pltpu.VMEM((ROWS, SAMPLES), jnp.bfloat16),
            pltpu.SemaphoreType.DMA((2,)),
        ],
        compiler_params=PARAMS,
        cost_estimate=cost(2 * 64 * SAMPLES * ROWS, 800_000),
        name="partial_spectra",
    )(kern, traces)


def slot_and_phase(route, low, high, offset, azimuth, trig):
    return pl.pallas_call(
        tables_kernel,
        out_shape=(
            jax.ShapeDtypeStruct((CAP, ROWS), jnp.bfloat16),
            jax.ShapeDtypeStruct((2, F_DEV, MIDS, MIDS), jnp.float32),
        ),
        in_specs=[VM, SM, SM, SM, SM, SM],
        out_specs=(VM, VM),
        compiler_params=PARAMS,
        cost_estimate=cost(2_000_000_000, 3_000_000),
        name="slot_and_phase",
    )(route, low, high, offset, azimuth, trig)


def place(part, slots, route, mid_x, mid_y):
    return pl.pallas_call(
        place_kernel,
        out_shape=jax.ShapeDtypeStruct((TILES, 16, CAP), jnp.bfloat16),
        in_specs=[VM] * 5,
        out_specs=VM,
        scratch_shapes=[pltpu.VMEM((TILES * 16, ROWS), jnp.bfloat16)],
        compiler_params=PARAMS,
        cost_estimate=cost(2 * 512 * ROWS * CAP, 1_000_000),
        name="place",
    )(part, slots, route, mid_x, mid_y)


def tile_image(got, table, tablet, phase):
    return pl.pallas_call(
        tile_kernel,
        out_shape=jax.ShapeDtypeStruct((F_DEV, MIDS, 2 * MIDS), jnp.float32),
        in_specs=[VM, ANY, ANY, ANY],
        out_specs=ANY,
        scratch_shapes=[
            pltpu.VMEM((COLS * MIDS, CHUNK * CAP), jnp.bfloat16),
            pltpu.VMEM((COLS * MIDS, CHUNK * CAP), jnp.bfloat16),
            pltpu.VMEM((MIDS, CHUNK * CAP), jnp.bfloat16),
            pltpu.VMEM((MIDS, CHUNK * CAP), jnp.bfloat16),
            pltpu.VMEM((COLS * MIDS, MIDS), jnp.float32),
            pltpu.VMEM((MIDS, MIDS), jnp.bfloat16),
            pltpu.VMEM((MIDS, MIDS), jnp.bfloat16),
            pltpu.VMEM((2, F_DEV, MIDS, MIDS), jnp.float32),
            pltpu.VMEM((F_DEV, MIDS, 2 * MIDS), jnp.float32),
            pltpu.SemaphoreType.DMA((3 + F_DEV,)),
        ],
        compiler_params=PARAMS,
        cost_estimate=cost(6_000_000_000, 5_000_000),
        name="tile_image",
    )(got, table, tablet, phase)


def per_device(traces, route, mid_x, mid_y, band_low, band_high, offset_bin, azimuth_bin):
    table = folded_table()
    route = route.reshape(1, ROWS)
    mid_x = mid_x.reshape(1, ROWS)
    mid_y = mid_y.reshape(1, ROWS)
    theta = azimuth_bin.astype(jnp.float32) * (math.pi / AZIMUTHS)
    trig = jnp.concatenate([jnp.cos(theta), jnp.sin(theta)])
    part = partial_spectra(jnp.asarray(time_kernel_blocks()), traces)
    part = lax.all_to_all(part, "band", split_axis=0, concat_axis=0, tiled=True)
    slots, phase = slot_and_phase(route, band_low, band_high, offset_bin, azimuth_bin, trig)
    sent = place(part, slots, route, mid_x, mid_y)
    got = lax.all_to_all(sent, "tile", split_axis=0, concat_axis=0, tiled=True)
    image = tile_image(got, jnp.asarray(table), jnp.asarray(np.ascontiguousarray(table.T)), phase)
    return image[None]


def solution(mesh):
    return jax.shard_map(
        per_device,
        mesh=mesh,
        in_specs=(
            P("tile", "band"),
            P("tile", None),
            P("tile"),
            P("tile"),
            P("tile"),
            P("tile"),
            P("tile"),
            P("tile"),
        ),
        out_specs=P("tile", "band", None, None),
        check_vma=False,
    )
```

```python
import math

import jax
import jax.numpy as jnp
import numpy as np
from jax import lax
from jax.experimental import pallas as pl
from jax.experimental.pallas import tpu as pltpu
from jax.sharding import PartitionSpec as P

MIDS = 256
HALF = 128
AZIMUTHS = 12
F_DEV = 4
COLS = 2 * F_DEV
BANDS = 8
TILES = 32
ROWS = 2048
SAMPLES = 128
NT = 1024
CAP = 128
ANCHOR = 64.0
LOG_SPAN = math.log((NT + ANCHOR) / ANCHOR)
CLASSES = 4
WIDE = MIDS // CLASSES
PARTS = 8
SPAN = CAP // PARTS
DEPTH = TILES * SPAN
PIECES = 1
PIECE = ROWS // PIECES
NT_DIMS = (((1,), (1,)), ((), ()))


def time_kernel_blocks():
    stretch = np.log((np.arange(NT) + ANCHOR) / ANCHOR)
    omegas = (np.arange(F_DEV * BANDS) + 1) * (2.0 * math.pi / LOG_SPAN)
    angles = omegas[:, None] * stretch[None, :]
    stacked = np.stack([np.cos(angles), -np.sin(angles)], axis=1) * NT**-0.5
    stacked = stacked.reshape(COLS * BANDS, BANDS, SAMPLES).transpose(1, 0, 2)
    return stacked.astype(np.float32).astype(jnp.bfloat16)


def folded_table():
    turns = (np.arange(MIDS)[:, None] * np.arange(HALF)[None, :]) % MIDS
    angles = turns * (2.0 * math.pi / MIDS)
    sines = np.sin(angles)
    sines[:, 0] = (-1.0) ** np.arange(MIDS)
    table = np.concatenate([np.cos(angles), sines], axis=1)
    return table.astype(np.float32).astype(jnp.bfloat16)


def sincos_turns(turns):
    quarters = (turns - jnp.round(turns)) * 4.0
    quadrant = jnp.round(quarters)
    angle = (quarters - quadrant) * (math.pi / 2)
    square = angle * angle
    sine = angle * (1.0 + square * (-1.0 / 6 + square * (1.0 / 120 + square * (-1.0 / 5040))))
    cosine = 1.0 + square * (
        -0.5 + square * (1.0 / 24 + square * (-1.0 / 720 + square * (1.0 / 40320)))
    )
    index = quadrant.astype(jnp.int32)
    odd = (index & 1) == 1
    low, high = jnp.where(odd, sine, cosine), jnp.where(odd, cosine, sine)
    cos_out = jnp.where(((index + 1) & 2) == 2, -low, low)
    sin_out = jnp.where((index & 2) == 2, -high, high)
    return cos_out, sin_out


def partial_kernel(kern_hbm, traces_hbm, out_hbm, kern, rows, part, sems):
    band = lax.axis_index("band")
    get_kern = pltpu.make_async_copy(kern_hbm.at[band], kern, sems.at[0])
    get_kern.start()
    gets, puts = [], []
    for q in range(PIECES):
        at = pl.ds(q * PIECE, PIECE)
        gets.append(pltpu.make_async_copy(traces_hbm.at[at], rows.at[at], sems.at[1 + q]))
        gets[q].start()
    get_kern.wait()
    for q in range(PIECES):
        gets[q].wait()
        piece = lax.dot_general(
            kern[...],
            rows[q * PIECE : (q + 1) * PIECE],
            NT_DIMS,
            preferred_element_type=jnp.float32,
        )
        lanes = pl.ds(q * PIECE // 2, PIECE // 2)
        for b in range(BANDS):
            block = piece[b * COLS : (b + 1) * COLS]
            part[b, :, q * PIECE // 2 : (q + 1) * PIECE // 2] = jnp.concatenate(
                [block[:, : PIECE // 2], block[:, PIECE // 2 :]], axis=0
            ).astype(jnp.bfloat16)
        puts.append(
            pltpu.make_async_copy(
                part.at[:, :, lanes], out_hbm.at[:, :, lanes], sems.at[1 + PIECES + q]
            )
        )
        puts[q].start()
    for put in puts:
        put.wait()


def signed_folded(shape, dim):
    index = lax.broadcasted_iota(jnp.int32, shape, dim)
    signed = jnp.where(index < HALF, index, jnp.where(index == HALF, -HALF, HALF - index))
    return signed.astype(jnp.float32) * (2.0 * math.pi / MIDS)


def slot_kernel(
    route_hbm, x_hbm, low_ref, high_ref, offset_ref, azimuth_ref, slot_ref, bins_ref, ints, sems
):
    copies = [
        pltpu.make_async_copy(route_hbm, ints.at[0], sems.at[0]),
        pltpu.make_async_copy(x_hbm, ints.at[1], sems.at[1]),
    ]
    for copy in copies:
        copy.start()
    block = MIDS
    row_i = lax.broadcasted_iota(jnp.int32, (block, block), 0)
    col_i = lax.broadcasted_iota(jnp.int32, (block, block), 1)
    upper = jnp.where(row_i < col_i, 1.0, 0.0).astype(jnp.bfloat16)
    class_i = lax.broadcasted_iota(jnp.int32, (CLASSES * TILES, block), 0)
    for i, ref in enumerate((low_ref, high_ref, offset_ref, azimuth_ref)):
        bins_ref[i] = jnp.full((8, 128), ref[0], jnp.int32)
    for copy in copies:
        copy.wait()
    cuts = [slice(step * block, (step + 1) * block) for step in range(ROWS // block)]
    members = []
    count = jnp.zeros((CLASSES * TILES, 1), jnp.float32)
    for cut in cuts:
        kind = (ints[1, :, cut] // WIDE) * TILES + ints[0, :, cut]
        members.append(jnp.where(class_i == kind, 1.0, 0.0))
        count = count + jnp.sum(members[-1], axis=1, keepdims=True)
    none = jnp.zeros((TILES, 1), jnp.float32)
    last = CAP - 1.0
    first = jnp.concatenate(
        [none, count[:TILES], last - count[3 * TILES :], none + last], axis=0
    )
    class_row = lax.broadcasted_iota(jnp.int32, (CLASSES * TILES, 1), 0)
    step_by = jnp.where(class_row < 2 * TILES, 1.0, -1.0)
    for cut, member in zip(cuts, members):
        earlier = jnp.dot(
            member.astype(jnp.bfloat16), upper, preferred_element_type=jnp.float32
        )
        slot = jnp.sum(member * (first + step_by * earlier), axis=0, keepdims=True)
        slot_ref[:, cut] = slot.astype(jnp.int32)
        first = first + step_by * jnp.sum(member, axis=1, keepdims=True)


def phase_kernel(bins_ref, sent_hbm, phase_ref):
    first = lax.axis_index("band") * F_DEV
    low, high, offset, azimuth = (bins_ref[i, :1, :1] for i in range(4))
    h = (offset.astype(jnp.float32) + 1.0) * 0.5
    cos_t, sin_t = sincos_turns(azimuth.astype(jnp.float32) * (0.5 / AZIMUTHS))
    kx = signed_folded((MIDS, MIDS), 0)
    ky = signed_folded((MIDS, MIDS), 1)
    inline = kx * (h * cos_t) + ky * (h * sin_t)
    along = signed_folded((MIDS, 128), 0) * h
    along = jnp.log1p(along * along)
    change = jnp.concatenate([along, along], axis=1) - jnp.log1p(inline * inline)
    unit = change * (0.5 / LOG_SPAN)
    turn_c, turn_s = sincos_turns(unit)
    cos_f, sin_f = sincos_turns(unit * (first + 1).astype(jnp.float32))
    scale = ROWS**-0.5 / MIDS
    for f in range(F_DEV):
        live = (first + f >= low) & (first + f < high)
        weight = jnp.where(live, scale, 0.0)
        phase_ref[0, f] = cos_f * weight
        phase_ref[1, f] = sin_f * weight
        if f + 1 < F_DEV:
            cos_f, sin_f = cos_f * turn_c - sin_f * turn_s, cos_f * turn_s + sin_f * turn_c


def place_kernel(
    part_hbm, rank_hbm, route_hbm, x_hbm, y_hbm, out_ref, part, ints, masked, sems
):
    copies = [
        pltpu.make_async_copy(src, ints.at[i], sems.at[i])
        for i, src in enumerate((rank_hbm, route_hbm, x_hbm, y_hbm))
    ]
    copies.append(pltpu.make_async_copy(part_hbm, part, sems.at[4]))
    for copy in copies:
        copy.start()
    for copy in copies[:4]:
        copy.wait()
    row = lax.broadcasted_iota(jnp.int32, (8, ROWS), 0)
    mids = jnp.where(
        row == 0,
        ints[2].astype(jnp.float32),
        jnp.where(row == 1, ints[3].astype(jnp.float32), jnp.where(row == 2, 1.0, 0.0)),
    )
    slot_i = lax.broadcasted_iota(jnp.int32, (CAP, ROWS), 0)
    slots = jnp.where(slot_i == ints[0], 1.0, 0.0).astype(jnp.bfloat16)
    tile = jnp.broadcast_to(ints[1], (16, ROWS))
    copies[4].wait()
    total = part[0].astype(jnp.float32)
    for b in range(1, BANDS):
        total = total + part[b].astype(jnp.float32)
    total = total.astype(jnp.bfloat16).astype(jnp.float32)
    lanes = [slice(q * PIECE // 2, (q + 1) * PIECE // 2) for q in range(PIECES)]
    spectra = jnp.concatenate(
        [total[h * COLS : (h + 1) * COLS, cut] for cut in lanes for h in range(2)], axis=1
    )
    values = jnp.concatenate([spectra, mids], axis=0)
    for g in range(TILES):
        masked[g * 16 : (g + 1) * 16, :] = jnp.where(tile == g, values, 0.0).astype(jnp.bfloat16)
    placed = lax.dot_general(masked[...], slots, NT_DIMS, preferred_element_type=jnp.float32)
    out_ref[...] = placed.astype(jnp.bfloat16).reshape(TILES, 16, CAP)


def tile_kernel(
    got_ref,
    table_hbm,
    tablet_hbm,
    phase_hbm,
    out_hbm,
    xa,
    xb,
    ya,
    yb,
    parts,
    cells,
    acc,
    table,
    tablet,
    phase,
    image,
    sems,
):
    copies = [
        pltpu.make_async_copy(table_hbm, table, sems.at[0]),
        pltpu.make_async_copy(tablet_hbm, tablet, sems.at[1]),
        pltpu.make_async_copy(phase_hbm, phase, sems.at[2]),
    ]
    for copy in copies:
        copy.start()
    lane_block = lax.broadcasted_iota(jnp.int32, (16, CAP), 1) // SPAN
    for i in range(TILES // PARTS):
        held = [got_ref[i * PARTS + k].astype(jnp.float32) for k in range(PARTS)]
        for d in (1, 2, 4):
            keep = (lane_block & d) == 0
            for k in range(PARTS):
                if k & d == 0:
                    a, b = held[k], held[k + d]
                    held[k] = jnp.where(keep, a, pltpu.roll(b, SPAN * d, 1))
                    held[k + d] = jnp.where(keep, pltpu.roll(a, CAP - SPAN * d, 1), b)
        for e in range(PARTS):
            parts[e, :, i * CAP : (i + 1) * CAP] = held[e].astype(jnp.bfloat16)
    parts[PARTS] = jnp.zeros((16, DEPTH), jnp.bfloat16)
    class_i = lax.broadcasted_iota(jnp.int32, (8, DEPTH), 0)
    bit_i = lax.broadcasted_iota(jnp.int32, (8, 1), 0)
    bits = jnp.zeros((8, 1), jnp.int32)
    for e in range(PARTS):
        tail = parts[e].astype(jnp.float32)
        kind = tail[COLS : COLS + 1].astype(jnp.int32) // WIDE
        hit = jnp.where((kind == class_i) & (tail[COLS + 2 : COLS + 3] > 0.5), 1.0, 0.0)
        found = jnp.max(hit, axis=1, keepdims=True).astype(jnp.int32)
        bits = bits + lax.shift_left(found, bit_i + CLASSES * e)
    mask = jnp.sum(jnp.where(bit_i < CLASSES, bits, 0))
    number = jnp.int32(0)
    for cell in range(PARTS * CLASSES):
        cells[number] = cell
        number = number + (lax.shift_right_logical(mask, jnp.int32(cell)) & 1)
    for extra in range(3):
        cells[number + extra] = PARTS * CLASSES

    iota = lax.broadcasted_iota(jnp.int32, (16, CAP), 0).astype(jnp.float32)
    one = jnp.ones((16, CAP), jnp.bfloat16)
    zero = jnp.zeros((16, CAP), jnp.bfloat16)

    def build(x_buf, y_buf, cell):
        part = cell // CLASSES
        start = ((cell % CLASSES) * WIDE).astype(jnp.float32)
        for i in range(DEPTH // CAP):
            cut = slice(i * CAP, (i + 1) * CAP)
            tail = parts[part, :, cut].astype(jnp.float32)
            rows = [
                jnp.broadcast_to(tail[c : c + 1], (16, CAP)).astype(jnp.bfloat16)
                for c in range(COLS + 2)
            ]
            for r in range(WIDE // 16):
                in_x = (iota + (start + 16.0 * r)).astype(jnp.bfloat16) == rows[COLS]
                for c in range(COLS):
                    at = c * WIDE + r * 16
                    x_buf[at : at + 16, cut] = jnp.where(in_x, rows[c], zero)
            for r in range(MIDS // 16):
                in_y = (iota + 16.0 * r).astype(jnp.bfloat16) == rows[COLS + 1]
                y_buf[r * 16 : (r + 1) * 16, cut] = jnp.where(in_y, one, zero)

    def add(x_buf, y_buf, cell):
        acc[cell % CLASSES] += lax.dot_general(
            x_buf[...], y_buf[...], NT_DIMS, preferred_element_type=jnp.float32
        )

    acc[...] = jnp.zeros_like(acc)
    build(xa, ya, cells[0])

    def pair(p, _):
        now, then, later = cells[2 * p], cells[2 * p + 1], cells[2 * p + 2]
        build(xb, yb, then)
        add(xa, ya, now)
        build(xa, ya, later)
        add(xb, yb, then)
        return 0

    lax.fori_loop(0, (number + 1) // 2, pair, 0)
    for copy in copies:
        copy.wait()

    lane0 = lax.broadcasted_iota(jnp.int32, (MIDS, HALF), 1) == 0
    bf = lambda v: v.astype(jnp.bfloat16)
    dot = lambda a, b: jnp.dot(a, b, preferred_element_type=jnp.float32)
    def stage_a(f):
        rows = [
            acc[q, c * WIDE : (c + 1) * WIDE]
            for c in (2 * f, 2 * f + 1)
            for q in range(CLASSES)
        ]
        u = dot(bf(jnp.concatenate(rows, axis=0)), table[...])
        cr, sr, ci, si = u[:MIDS, :HALF], u[:MIDS, HALF:], u[MIDS:, :HALF], u[MIDS:, HALF:]
        h_r = [jnp.where(lane0, cr, cr + si), jnp.where(lane0, sr, cr - si)]
        h_i = [jnp.where(lane0, ci, ci - sr), jnp.where(lane0, si, ci + sr)]
        return bf(jnp.concatenate(h_r + h_i, axis=1))

    top0 = lax.broadcasted_iota(jnp.int32, (8, MIDS), 0) == 0

    def pick_row0(zero_row, rest):
        return jnp.concatenate([jnp.where(top0, zero_row[:8], rest[:8]), rest[8:]], axis=0)

    def stage_b(f, h):
        v = dot(tablet[...], h)
        cr, sr, ci, si = v[:HALF, :MIDS], v[HALF:, :MIDS], v[:HALF, MIDS:], v[HALF:, MIDS:]
        wpr, wpi = pick_row0(cr, cr + si), pick_row0(ci, ci - sr)
        wmr, wmi = pick_row0(sr, cr - si), pick_row0(si, ci + sr)
        pc, ps = phase[0, f, :HALF], phase[1, f, :HALF]
        mc, ms = phase[0, f, HALF:], phase[1, f, HALF:]
        mpr, mpi = wpr * pc - wpi * ps, wpr * ps + wpi * pc
        mmr, mmi = wmr * mc - wmi * ms, wmr * ms + wmi * mc
        a_r, a_i = pick_row0(mpr, mpr + mmr), pick_row0(mpi, mpi + mmi)
        d_r, d_i = pick_row0(mmr, mmi - mpi), pick_row0(mmi, mpr - mmr)
        return bf(
            jnp.concatenate(
                [jnp.concatenate([a_r, a_i], axis=1), jnp.concatenate([d_r, d_i], axis=1)],
                axis=0,
            )
        )

    def stage_c(f, folded):
        q = dot(table[...], folded)
        qpr, qmr = q[:, :HALF], q[:, HALF:MIDS]
        qpi, qmi = q[:, MIDS : MIDS + HALF], q[:, MIDS + HALF :]
        a_r = jnp.where(lane0, qpr, qpr + qmr)
        a_i = jnp.where(lane0, qpi, qpi + qmi)
        d_r = jnp.where(lane0, qmr, qmi - qpi)
        d_i = jnp.where(lane0, qmi, qpr - qmr)
        return bf(
            jnp.concatenate(
                [jnp.concatenate([a_r, d_r], axis=1), jnp.concatenate([a_i, d_i], axis=1)],
                axis=0,
            )
        )

    def stage_d(f, folded):
        w = dot(folded, tablet[...])
        image[f, :, :MIDS] = w[:MIDS]
        image[f, :, MIDS:] = w[MIDS:]
        put = pltpu.make_async_copy(image.at[f], out_hbm.at[f], sems.at[3 + f])
        put.start()
        puts.append(put)

    puts = []
    stages = (stage_b, stage_c, stage_d)
    held = {}
    for step in range(F_DEV + 3):
        for f in range(F_DEV):
            if f == step:
                held[f] = stage_a(f)
            elif 0 < step - f <= 3:
                held[f] = stages[step - f - 1](f, held[f])
    for put in puts:
        put.wait()


VM = pl.BlockSpec(memory_space=pltpu.VMEM)
SM = pl.BlockSpec(memory_space=pltpu.SMEM)
ANY = pl.BlockSpec(memory_space=pl.ANY)


def vmem(mib):
    return pltpu.CompilerParams(vmem_limit_bytes=mib * 1024 * 1024)


def cost(flops, moved):
    return pl.CostEstimate(flops=flops, bytes_accessed=moved, transcendentals=0)


def partial_spectra(kern, traces):
    return pl.pallas_call(
        partial_kernel,
        out_shape=jax.ShapeDtypeStruct((BANDS, 16, ROWS // 2), jnp.bfloat16),
        in_specs=[ANY, ANY],
        out_specs=ANY,
        scratch_shapes=[
            pltpu.VMEM((COLS * BANDS, SAMPLES), jnp.bfloat16),
            pltpu.VMEM((ROWS, SAMPLES), jnp.bfloat16),
            pltpu.VMEM((BANDS, 16, ROWS // 2), jnp.bfloat16),
            pltpu.SemaphoreType.DMA((1 + 2 * PIECES,)),
        ],
        compiler_params=vmem(60),
        cost_estimate=cost(2 * 64 * SAMPLES * ROWS, 800_000),
        name="partial_spectra",
    )(kern, traces)


def slot_ranks(route, mid_x, low, high, offset, azimuth):
    return pl.pallas_call(
        slot_kernel,
        out_shape=(
            jax.ShapeDtypeStruct((1, ROWS), jnp.int32),
            jax.ShapeDtypeStruct((4, 8, 128), jnp.int32),
        ),
        in_specs=[ANY] * 2 + [SM] * 4,
        out_specs=(VM, VM),
        scratch_shapes=[pltpu.VMEM((2, 1, ROWS), jnp.int32), pltpu.SemaphoreType.DMA((2,))],
        compiler_params=vmem(8),
        cost_estimate=cost(2_000_000_000, 3_000_000),
        name="slot_ranks",
    )(route, mid_x, low, high, offset, azimuth)


def phase_table(bins, sent):
    return pl.pallas_call(
        phase_kernel,
        out_shape=jax.ShapeDtypeStruct((2, F_DEV, MIDS, MIDS), jnp.float32),
        in_specs=[VM, ANY],
        out_specs=VM,
        compiler_params=vmem(16),
        cost_estimate=cost(2_000_000_000, 3_000_000),
        name="phase_table",
    )(bins, sent)


def place(part, rank, route, mid_x, mid_y):
    return pl.pallas_call(
        place_kernel,
        out_shape=jax.ShapeDtypeStruct((TILES, 16, CAP), jnp.bfloat16),
        in_specs=[ANY] * 5,
        out_specs=VM,
        scratch_shapes=[
            pltpu.VMEM((BANDS, 16, ROWS // 2), jnp.bfloat16),
            pltpu.VMEM((4, 1, ROWS), jnp.int32),
            pltpu.VMEM((TILES * 16, ROWS), jnp.bfloat16),
            pltpu.SemaphoreType.DMA((5,)),
        ],
        compiler_params=vmem(16),
        cost_estimate=cost(2 * 512 * ROWS * CAP, 1_000_000),
        name="place",
    )(part, rank, route, mid_x, mid_y)


def tile_image(got, table, tablet, phase):
    return pl.pallas_call(
        tile_kernel,
        out_shape=jax.ShapeDtypeStruct((F_DEV, MIDS, 2 * MIDS), jnp.float32),
        in_specs=[VM, ANY, ANY, ANY],
        out_specs=ANY,
        scratch_shapes=[
            pltpu.VMEM((COLS * WIDE, DEPTH), jnp.bfloat16),
            pltpu.VMEM((COLS * WIDE, DEPTH), jnp.bfloat16),
            pltpu.VMEM((MIDS, DEPTH), jnp.bfloat16),
            pltpu.VMEM((MIDS, DEPTH), jnp.bfloat16),
            pltpu.VMEM((PARTS + 1, 16, DEPTH), jnp.bfloat16),
            pltpu.SMEM((PARTS * CLASSES + 8,), jnp.int32),
            pltpu.VMEM((CLASSES, COLS * WIDE, MIDS), jnp.float32),
            pltpu.VMEM((MIDS, MIDS), jnp.bfloat16),
            pltpu.VMEM((MIDS, MIDS), jnp.bfloat16),
            pltpu.VMEM((2, F_DEV, MIDS, MIDS), jnp.float32),
            pltpu.VMEM((F_DEV, MIDS, 2 * MIDS), jnp.float32),
            pltpu.SemaphoreType.DMA((3 + F_DEV,)),
        ],
        compiler_params=vmem(32),
        cost_estimate=cost(6_000_000_000, 5_000_000),
        name="tile_image",
    )(got, table, tablet, phase)


def per_device(traces, route, mid_x, mid_y, band_low, band_high, offset_bin, azimuth_bin):
    table = folded_table()
    route = route.reshape(1, ROWS)
    mid_x = mid_x.reshape(1, ROWS)
    mid_y = mid_y.reshape(1, ROWS)
    part = partial_spectra(jnp.asarray(time_kernel_blocks()), traces)
    part = lax.all_to_all(part, "band", split_axis=0, concat_axis=0, tiled=True)
    rank, bins = slot_ranks(route, mid_x, band_low, band_high, offset_bin, azimuth_bin)
    sent = place(part, rank, route, mid_x, mid_y)
    got = lax.all_to_all(sent, "tile", split_axis=0, concat_axis=0, tiled=True)
    phase = phase_table(bins, sent)
    image = tile_image(got, jnp.asarray(table), jnp.asarray(np.ascontiguousarray(table.T)), phase)
    return image[None]


def solution(mesh):
    return jax.shard_map(
        per_device,
        mesh=mesh,
        in_specs=(
            P("tile", "band"),
            P("tile", None),
            P("tile"),
            P("tile"),
            P("tile"),
            P("tile"),
            P("tile"),
            P("tile"),
        ),
        out_specs=P("tile", "band", None, None),
        check_vma=False,
    )
```

```python
import math

import jax
import jax.numpy as jnp
import numpy as np
from jax import lax
from jax.experimental import pallas as pl
from jax.experimental.pallas import tpu as pltpu
from jax.sharding import PartitionSpec as P

MIDS = 256
HALF = 128
AZIMUTHS = 12
F_DEV = 4
COLS = 2 * F_DEV
BANDS = 8
TILES = 32
ROWS = 2048
SAMPLES = 128
NT = 1024
CAP = 128
ANCHOR = 64.0
LOG_SPAN = math.log((NT + ANCHOR) / ANCHOR)
CLASSES = 4
WIDE = MIDS // CLASSES
PARTS = 8
SPAN = CAP // PARTS
DEPTH = TILES * SPAN
UNROLL = 16
PIECES = 1
PIECE = ROWS // PIECES
NT_DIMS = (((1,), (1,)), ((), ()))


def time_kernel_blocks():
    stretch = np.log((np.arange(NT) + ANCHOR) / ANCHOR)
    omegas = (np.arange(F_DEV * BANDS) + 1) * (2.0 * math.pi / LOG_SPAN)
    angles = omegas[:, None] * stretch[None, :]
    stacked = np.stack([np.cos(angles), -np.sin(angles)], axis=1) * NT**-0.5
    stacked = stacked.reshape(COLS * BANDS, BANDS, SAMPLES).transpose(1, 0, 2)
    return stacked.astype(np.float32).astype(jnp.bfloat16)


def folded_table():
    turns = (np.arange(MIDS)[:, None] * np.arange(HALF)[None, :]) % MIDS
    angles = turns * (2.0 * math.pi / MIDS)
    sines = np.sin(angles)
    sines[:, 0] = (-1.0) ** np.arange(MIDS)
    table = np.concatenate([np.cos(angles), sines], axis=1)
    return table.astype(np.float32).astype(jnp.bfloat16)


def sincos_turns(turns):
    quarters = (turns - jnp.round(turns)) * 4.0
    quadrant = jnp.round(quarters)
    angle = (quarters - quadrant) * (math.pi / 2)
    square = angle * angle
    sine = angle * (1.0 + square * (-1.0 / 6 + square * (1.0 / 120 + square * (-1.0 / 5040))))
    cosine = 1.0 + square * (
        -0.5 + square * (1.0 / 24 + square * (-1.0 / 720 + square * (1.0 / 40320)))
    )
    index = quadrant.astype(jnp.int32)
    odd = (index & 1) == 1
    low, high = jnp.where(odd, sine, cosine), jnp.where(odd, cosine, sine)
    cos_out = jnp.where(((index + 1) & 2) == 2, -low, low)
    sin_out = jnp.where((index & 2) == 2, -high, high)
    return cos_out, sin_out


def partial_kernel(kern_hbm, traces_hbm, out_hbm, kern, rows, part, sems):
    band = lax.axis_index("band")
    get_kern = pltpu.make_async_copy(kern_hbm.at[band], kern, sems.at[0])
    get_kern.start()
    gets, puts = [], []
    for q in range(PIECES):
        at = pl.ds(q * PIECE, PIECE)
        gets.append(pltpu.make_async_copy(traces_hbm.at[at], rows.at[at], sems.at[1 + q]))
        gets[q].start()
    get_kern.wait()
    for q in range(PIECES):
        gets[q].wait()
        piece = lax.dot_general(
            kern[...],
            rows[q * PIECE : (q + 1) * PIECE],
            NT_DIMS,
            preferred_element_type=jnp.float32,
        )
        lanes = pl.ds(q * PIECE // 2, PIECE // 2)
        for b in range(BANDS):
            block = piece[b * COLS : (b + 1) * COLS]
            part[b, :, q * PIECE // 2 : (q + 1) * PIECE // 2] = jnp.concatenate(
                [block[:, : PIECE // 2], block[:, PIECE // 2 :]], axis=0
            ).astype(jnp.bfloat16)
        puts.append(
            pltpu.make_async_copy(
                part.at[:, :, lanes], out_hbm.at[:, :, lanes], sems.at[1 + PIECES + q]
            )
        )
        puts[q].start()
    for put in puts:
        put.wait()


def signed_folded(shape, dim):
    index = lax.broadcasted_iota(jnp.int32, shape, dim)
    signed = jnp.where(index < HALF, index, jnp.where(index == HALF, -HALF, HALF - index))
    return signed.astype(jnp.float32) * (2.0 * math.pi / MIDS)


def slot_kernel(
    route_hbm, x_hbm, low_ref, high_ref, offset_ref, azimuth_ref, slot_ref, bins_ref, ints, sems
):
    copies = [
        pltpu.make_async_copy(route_hbm, ints.at[0], sems.at[0]),
        pltpu.make_async_copy(x_hbm, ints.at[1], sems.at[1]),
    ]
    for copy in copies:
        copy.start()
    block = MIDS
    row_i = lax.broadcasted_iota(jnp.int32, (block, block), 0)
    col_i = lax.broadcasted_iota(jnp.int32, (block, block), 1)
    upper = jnp.where(row_i < col_i, 1.0, 0.0).astype(jnp.bfloat16)
    class_i = lax.broadcasted_iota(jnp.int32, (CLASSES * TILES, block), 0)
    for i, ref in enumerate((low_ref, high_ref, offset_ref, azimuth_ref)):
        bins_ref[i] = jnp.full((8, 128), ref[0], jnp.int32)
    for copy in copies:
        copy.wait()
    cuts = [slice(step * block, (step + 1) * block) for step in range(ROWS // block)]
    members = []
    count = jnp.zeros((CLASSES * TILES, 1), jnp.float32)
    for cut in cuts:
        kind = (ints[1, :, cut] // WIDE) * TILES + ints[0, :, cut]
        members.append(jnp.where(class_i == kind, 1.0, 0.0))
        count = count + jnp.sum(members[-1], axis=1, keepdims=True)
    none = jnp.zeros((TILES, 1), jnp.float32)
    last = CAP - 1.0
    first = jnp.concatenate(
        [none, count[:TILES], last - count[3 * TILES :], none + last], axis=0
    )
    class_row = lax.broadcasted_iota(jnp.int32, (CLASSES * TILES, 1), 0)
    step_by = jnp.where(class_row < 2 * TILES, 1.0, -1.0)
    for cut, member in zip(cuts, members):
        earlier = jnp.dot(
            member.astype(jnp.bfloat16), upper, preferred_element_type=jnp.float32
        )
        slot = jnp.sum(member * (first + step_by * earlier), axis=0, keepdims=True)
        slot_ref[:, cut] = slot.astype(jnp.int32)
        first = first + step_by * jnp.sum(member, axis=1, keepdims=True)


def phase_kernel(bins_ref, sent_hbm, phase_ref):
    first = lax.axis_index("band") * F_DEV
    low, high, offset, azimuth = (bins_ref[i, :1, :1] for i in range(4))
    h = (offset.astype(jnp.float32) + 1.0) * 0.5
    cos_t, sin_t = sincos_turns(azimuth.astype(jnp.float32) * (0.5 / AZIMUTHS))
    kx = signed_folded((MIDS, MIDS), 0)
    ky = signed_folded((MIDS, MIDS), 1)
    inline = kx * (h * cos_t) + ky * (h * sin_t)
    along = signed_folded((MIDS, 128), 0) * h
    along = jnp.log1p(along * along)
    change = jnp.concatenate([along, along], axis=1) - jnp.log1p(inline * inline)
    unit = change * (0.5 / LOG_SPAN)
    turn_c, turn_s = sincos_turns(unit)
    cos_f, sin_f = sincos_turns(unit * (first + 1).astype(jnp.float32))
    scale = ROWS**-0.5 / MIDS
    for f in range(F_DEV):
        live = (first + f >= low) & (first + f < high)
        weight = jnp.where(live, scale, 0.0)
        phase_ref[0, f] = cos_f * weight
        phase_ref[1, f] = sin_f * weight
        if f + 1 < F_DEV:
            cos_f, sin_f = cos_f * turn_c - sin_f * turn_s, cos_f * turn_s + sin_f * turn_c


def place_kernel(part_ref, rank_ref, route_ref, x_ref, y_ref, out_ref, masked):
    row = lax.broadcasted_iota(jnp.int32, (8, ROWS), 0)
    mids = jnp.where(
        row == 0,
        x_ref[...].astype(jnp.float32),
        jnp.where(row == 1, y_ref[...].astype(jnp.float32), jnp.where(row == 2, 1.0, 0.0)),
    )
    slot_i = lax.broadcasted_iota(jnp.int32, (CAP, ROWS), 0)
    slots = jnp.where(slot_i == rank_ref[...], 1.0, 0.0).astype(jnp.bfloat16)
    tile = jnp.broadcast_to(route_ref[...], (16, ROWS))
    total = part_ref[0].astype(jnp.float32)
    for b in range(1, BANDS):
        total = total + part_ref[b].astype(jnp.float32)
    total = total.astype(jnp.bfloat16).astype(jnp.float32)
    lanes = [slice(q * PIECE // 2, (q + 1) * PIECE // 2) for q in range(PIECES)]
    spectra = jnp.concatenate(
        [total[h * COLS : (h + 1) * COLS, cut] for cut in lanes for h in range(2)], axis=1
    )
    values = jnp.concatenate([spectra, mids], axis=0)
    for g in range(TILES):
        masked[g * 16 : (g + 1) * 16, :] = jnp.where(tile == g, values, 0.0).astype(jnp.bfloat16)
    placed = lax.dot_general(masked[...], slots, NT_DIMS, preferred_element_type=jnp.float32)
    out_ref[...] = placed.astype(jnp.bfloat16).reshape(TILES, 16, CAP)


def tile_kernel(
    got_ref,
    table_hbm,
    tablet_hbm,
    phase_hbm,
    out_hbm,
    xa,
    xb,
    ya,
    yb,
    parts,
    cells,
    acc,
    table,
    tablet,
    phase,
    image,
    sems,
):
    copies = [
        pltpu.make_async_copy(table_hbm, table, sems.at[0]),
        pltpu.make_async_copy(tablet_hbm, tablet, sems.at[1]),
        pltpu.make_async_copy(phase_hbm, phase, sems.at[2]),
    ]
    for copy in copies:
        copy.start()
    lane_block = lax.broadcasted_iota(jnp.int32, (16, CAP), 1) // SPAN
    for i in range(TILES // PARTS):
        held = [got_ref[i * PARTS + k].astype(jnp.float32) for k in range(PARTS)]
        for d in (1, 2, 4):
            keep = (lane_block & d) == 0
            for k in range(PARTS):
                if k & d == 0:
                    a, b = held[k], held[k + d]
                    held[k] = jnp.where(keep, a, pltpu.roll(b, SPAN * d, 1))
                    held[k + d] = jnp.where(keep, pltpu.roll(a, CAP - SPAN * d, 1), b)
        for e in range(PARTS):
            parts[e, :, i * CAP : (i + 1) * CAP] = held[e].astype(jnp.bfloat16)
    parts[PARTS] = jnp.zeros((16, DEPTH), jnp.bfloat16)
    class_i = lax.broadcasted_iota(jnp.int32, (8, DEPTH), 0)
    bit_i = lax.broadcasted_iota(jnp.int32, (8, 1), 0)
    bits = jnp.zeros((8, 1), jnp.int32)
    for e in range(PARTS):
        tail = parts[e].astype(jnp.float32)
        kind = tail[COLS : COLS + 1].astype(jnp.int32) // WIDE
        hit = jnp.where((kind == class_i) & (tail[COLS + 2 : COLS + 3] > 0.5), 1.0, 0.0)
        found = jnp.max(hit, axis=1, keepdims=True).astype(jnp.int32)
        bits = bits + lax.shift_left(found, bit_i + CLASSES * e)
    mask = jnp.sum(jnp.where(bit_i < CLASSES, bits, 0))
    number = jnp.int32(0)
    for cell in range(PARTS * CLASSES):
        cells[number] = cell
        number = number + (lax.shift_right_logical(mask, jnp.int32(cell)) & 1)
    for extra in range(UNROLL + 1):
        cells[number + extra] = PARTS * CLASSES

    iota = lax.broadcasted_iota(jnp.int32, (16, CAP), 0).astype(jnp.float32)
    one = jnp.ones((16, CAP), jnp.bfloat16)
    zero = jnp.zeros((16, CAP), jnp.bfloat16)

    def build(x_buf, y_buf, cell):
        part = cell // CLASSES
        start = ((cell % CLASSES) * WIDE).astype(jnp.float32)
        for i in range(DEPTH // CAP):
            cut = slice(i * CAP, (i + 1) * CAP)
            tail = parts[part, :, cut].astype(jnp.float32)
            rows = [
                jnp.broadcast_to(tail[c : c + 1], (16, CAP)).astype(jnp.bfloat16)
                for c in range(COLS + 2)
            ]
            for r in range(WIDE // 16):
                in_x = (iota + (start + 16.0 * r)).astype(jnp.bfloat16) == rows[COLS]
                for c in range(COLS):
                    at = c * WIDE + r * 16
                    x_buf[at : at + 16, cut] = jnp.where(in_x, rows[c], zero)
            for r in range(MIDS // 16):
                in_y = (iota + 16.0 * r).astype(jnp.bfloat16) == rows[COLS + 1]
                y_buf[r * 16 : (r + 1) * 16, cut] = jnp.where(in_y, one, zero)

    def add(x_buf, y_buf, cell):
        acc[cell % CLASSES] += lax.dot_general(
            x_buf[...], y_buf[...], NT_DIMS, preferred_element_type=jnp.float32
        )

    acc[...] = jnp.zeros_like(acc)
    build(xa, ya, cells[0])

    def many(p, _):
        for k in range(UNROLL):
            here, there = ((xa, ya), (xb, yb))[:: 1 if k % 2 == 0 else -1]
            build(*there, cells[UNROLL * p + k + 1])
            add(*here, cells[UNROLL * p + k])
        return 0

    lax.fori_loop(0, (number + UNROLL - 1) // UNROLL, many, 0)
    for copy in copies:
        copy.wait()

    lane0 = lax.broadcasted_iota(jnp.int32, (MIDS, HALF), 1) == 0
    bf = lambda v: v.astype(jnp.bfloat16)
    dot = lambda a, b: jnp.dot(a, b, preferred_element_type=jnp.float32)
    def stage_a(f):
        rows = [
            acc[q, c * WIDE : (c + 1) * WIDE]
            for c in (2 * f, 2 * f + 1)
            for q in range(CLASSES)
        ]
        u = dot(bf(jnp.concatenate(rows, axis=0)), table[...])
        cr, sr, ci, si = u[:MIDS, :HALF], u[:MIDS, HALF:], u[MIDS:, :HALF], u[MIDS:, HALF:]
        h_r = [jnp.where(lane0, cr, cr + si), jnp.where(lane0, sr, cr - si)]
        h_i = [jnp.where(lane0, ci, ci - sr), jnp.where(lane0, si, ci + sr)]
        return bf(jnp.concatenate(h_r + h_i, axis=1))

    top0 = lax.broadcasted_iota(jnp.int32, (8, MIDS), 0) == 0

    def pick_row0(zero_row, rest):
        return jnp.concatenate([jnp.where(top0, zero_row[:8], rest[:8]), rest[8:]], axis=0)

    def stage_b(f, h):
        v = dot(tablet[...], h)
        cr, sr, ci, si = v[:HALF, :MIDS], v[HALF:, :MIDS], v[:HALF, MIDS:], v[HALF:, MIDS:]
        wpr, wpi = pick_row0(cr, cr + si), pick_row0(ci, ci - sr)
        wmr, wmi = pick_row0(sr, cr - si), pick_row0(si, ci + sr)
        pc, ps = phase[0, f, :HALF], phase[1, f, :HALF]
        mc, ms = phase[0, f, HALF:], phase[1, f, HALF:]
        mpr, mpi = wpr * pc - wpi * ps, wpr * ps + wpi * pc
        mmr, mmi = wmr * mc - wmi * ms, wmr * ms + wmi * mc
        a_r, a_i = pick_row0(mpr, mpr + mmr), pick_row0(mpi, mpi + mmi)
        d_r, d_i = pick_row0(mmr, mmi - mpi), pick_row0(mmi, mpr - mmr)
        return bf(
            jnp.concatenate(
                [jnp.concatenate([a_r, a_i], axis=1), jnp.concatenate([d_r, d_i], axis=1)],
                axis=0,
            )
        )

    def stage_c(f, folded):
        q = dot(table[...], folded)
        qpr, qmr = q[:, :HALF], q[:, HALF:MIDS]
        qpi, qmi = q[:, MIDS : MIDS + HALF], q[:, MIDS + HALF :]
        a_r = jnp.where(lane0, qpr, qpr + qmr)
        a_i = jnp.where(lane0, qpi, qpi + qmi)
        d_r = jnp.where(lane0, qmr, qmi - qpi)
        d_i = jnp.where(lane0, qmi, qpr - qmr)
        return bf(
            jnp.concatenate(
                [jnp.concatenate([a_r, d_r], axis=1), jnp.concatenate([a_i, d_i], axis=1)],
                axis=0,
            )
        )

    def stage_d(f, folded):
        for i in range(2):
            cut = slice(i * MIDS, (i + 1) * MIDS)
            image[f, :, cut] = dot(folded[cut], tablet[...])
            put = pltpu.make_async_copy(
                image.at[f, :, cut], out_hbm.at[f, :, cut], sems.at[3 + 2 * f + i]
            )
            put.start()
            puts.append(put)

    puts = []
    stages = (stage_b, stage_c, stage_d)
    held = {}
    for step in range(5):
        for g in range(2):
            for f in (2 * g, 2 * g + 1):
                if g == step:
                    held[f] = stage_a(f)
                elif 0 < step - g <= 3:
                    held[f] = stages[step - g - 1](f, held[f])
    for put in puts:
        put.wait()


VM = pl.BlockSpec(memory_space=pltpu.VMEM)
SM = pl.BlockSpec(memory_space=pltpu.SMEM)
ANY = pl.BlockSpec(memory_space=pl.ANY)


def vmem(mib):
    return pltpu.CompilerParams(vmem_limit_bytes=mib * 1024 * 1024)


def cost(flops, moved):
    return pl.CostEstimate(flops=flops, bytes_accessed=moved, transcendentals=0)


def partial_spectra(kern, traces):
    return pl.pallas_call(
        partial_kernel,
        out_shape=jax.ShapeDtypeStruct((BANDS, 16, ROWS // 2), jnp.bfloat16),
        in_specs=[ANY, ANY],
        out_specs=ANY,
        scratch_shapes=[
            pltpu.VMEM((COLS * BANDS, SAMPLES), jnp.bfloat16),
            pltpu.VMEM((ROWS, SAMPLES), jnp.bfloat16),
            pltpu.VMEM((BANDS, 16, ROWS // 2), jnp.bfloat16),
            pltpu.SemaphoreType.DMA((1 + 2 * PIECES,)),
        ],
        compiler_params=vmem(60),
        cost_estimate=cost(2 * 64 * SAMPLES * ROWS, 800_000),
        name="partial_spectra",
    )(kern, traces)


def slot_ranks(route, mid_x, low, high, offset, azimuth):
    return pl.pallas_call(
        slot_kernel,
        out_shape=(
            jax.ShapeDtypeStruct((1, ROWS), jnp.int32),
            jax.ShapeDtypeStruct((4, 8, 128), jnp.int32),
        ),
        in_specs=[ANY] * 2 + [SM] * 4,
        out_specs=(VM, VM),
        scratch_shapes=[pltpu.VMEM((2, 1, ROWS), jnp.int32), pltpu.SemaphoreType.DMA((2,))],
        compiler_params=vmem(8),
        cost_estimate=cost(2_000_000_000, 3_000_000),
        name="slot_ranks",
    )(route, mid_x, low, high, offset, azimuth)


def phase_table(bins, sent):
    return pl.pallas_call(
        phase_kernel,
        out_shape=jax.ShapeDtypeStruct((2, F_DEV, MIDS, MIDS), jnp.float32),
        in_specs=[VM, ANY],
        out_specs=VM,
        compiler_params=vmem(16),
        cost_estimate=cost(2_000_000_000, 3_000_000),
        name="phase_table",
    )(bins, sent)


def place(part, rank, route, mid_x, mid_y):
    return pl.pallas_call(
        place_kernel,
        out_shape=jax.ShapeDtypeStruct((TILES, 16, CAP), jnp.bfloat16),
        in_specs=[VM] * 5,
        out_specs=VM,
        scratch_shapes=[
            pltpu.VMEM((TILES * 16, ROWS), jnp.bfloat16),
        ],
        compiler_params=vmem(16),
        cost_estimate=cost(2 * 512 * ROWS * CAP, 1_000_000),
        name="place",
    )(part, rank, route, mid_x, mid_y)


def tile_image(got, table, tablet, phase):
    return pl.pallas_call(
        tile_kernel,
        out_shape=jax.ShapeDtypeStruct((F_DEV, MIDS, 2 * MIDS), jnp.float32),
        in_specs=[VM, ANY, ANY, ANY],
        out_specs=ANY,
        scratch_shapes=[
            pltpu.VMEM((COLS * WIDE, DEPTH), jnp.bfloat16),
            pltpu.VMEM((COLS * WIDE, DEPTH), jnp.bfloat16),
            pltpu.VMEM((MIDS, DEPTH), jnp.bfloat16),
            pltpu.VMEM((MIDS, DEPTH), jnp.bfloat16),
            pltpu.VMEM((PARTS + 1, 16, DEPTH), jnp.bfloat16),
            pltpu.SMEM((PARTS * CLASSES + UNROLL + 2,), jnp.int32),
            pltpu.VMEM((CLASSES, COLS * WIDE, MIDS), jnp.float32),
            pltpu.VMEM((MIDS, MIDS), jnp.bfloat16),
            pltpu.VMEM((MIDS, MIDS), jnp.bfloat16),
            pltpu.VMEM((2, F_DEV, MIDS, MIDS), jnp.float32),
            pltpu.VMEM((F_DEV, MIDS, 2 * MIDS), jnp.float32),
            pltpu.SemaphoreType.DMA((3 + 2 * F_DEV,)),
        ],
        compiler_params=vmem(32),
        cost_estimate=cost(6_000_000_000, 5_000_000),
        name="tile_image",
    )(got, table, tablet, phase)


def per_device(traces, route, mid_x, mid_y, band_low, band_high, offset_bin, azimuth_bin):
    table = folded_table()
    route = route.reshape(1, ROWS)
    mid_x = mid_x.reshape(1, ROWS)
    mid_y = mid_y.reshape(1, ROWS)
    part = partial_spectra(jnp.asarray(time_kernel_blocks()), traces)
    part = lax.all_to_all(part, "band", split_axis=0, concat_axis=0, tiled=True)
    rank, bins = slot_ranks(route, mid_x, band_low, band_high, offset_bin, azimuth_bin)
    sent = place(part, rank, route, mid_x, mid_y)
    got = lax.all_to_all(sent, "tile", split_axis=0, concat_axis=0, tiled=True)
    phase = phase_table(bins, sent)
    image = tile_image(got, jnp.asarray(table), jnp.asarray(np.ascontiguousarray(table.T)), phase)
    return image[None]


def solution(mesh):
    return jax.shard_map(
        per_device,
        mesh=mesh,
        in_specs=(
            P("tile", "band"),
            P("tile", None),
            P("tile"),
            P("tile"),
            P("tile"),
            P("tile"),
            P("tile"),
            P("tile"),
        ),
        out_specs=P("tile", "band", None, None),
        check_vma=False,
    )
```

```python
import math

import jax
import jax.numpy as jnp
import numpy as np
from jax import lax
from jax.experimental import pallas as pl
from jax.experimental.pallas import tpu as pltpu
from jax.sharding import PartitionSpec as P

MIDS = 256
HALF = 128
AZIMUTHS = 12
F_DEV = 4
COLS = 2 * F_DEV
BANDS = 8
TILES = 32
ROWS = 2048
SAMPLES = 128
NT = 1024
CAP = 128
ANCHOR = 64.0
LOG_SPAN = math.log((NT + ANCHOR) / ANCHOR)
CLASSES = 4
WIDE = MIDS // CLASSES
PARTS = 8
SPAN = CAP // PARTS
DEPTH = TILES * SPAN
FIRST = 16
MORE = 4
PIECES = 1
PIECE = ROWS // PIECES
NT_DIMS = (((1,), (1,)), ((), ()))


def time_kernel_blocks():
    stretch = np.log((np.arange(NT) + ANCHOR) / ANCHOR)
    omegas = (np.arange(F_DEV * BANDS) + 1) * (2.0 * math.pi / LOG_SPAN)
    angles = omegas[:, None] * stretch[None, :]
    stacked = np.stack([np.cos(angles), -np.sin(angles)], axis=1) * NT**-0.5
    stacked = stacked.reshape(COLS * BANDS, BANDS, SAMPLES).transpose(1, 0, 2)
    return stacked.astype(np.float32).astype(jnp.bfloat16)


def folded_table():
    turns = (np.arange(MIDS)[:, None] * np.arange(HALF)[None, :]) % MIDS
    angles = turns * (2.0 * math.pi / MIDS)
    sines = np.sin(angles)
    sines[:, 0] = (-1.0) ** np.arange(MIDS)
    table = np.concatenate([np.cos(angles), sines], axis=1)
    return table.astype(np.float32).astype(jnp.bfloat16)


def sincos_turns(turns):
    quarters = (turns - jnp.round(turns)) * 4.0
    quadrant = jnp.round(quarters)
    angle = (quarters - quadrant) * (math.pi / 2)
    square = angle * angle
    sine = angle * (1.0 + square * (-1.0 / 6 + square * (1.0 / 120 + square * (-1.0 / 5040))))
    cosine = 1.0 + square * (
        -0.5 + square * (1.0 / 24 + square * (-1.0 / 720 + square * (1.0 / 40320)))
    )
    index = quadrant.astype(jnp.int32)
    odd = (index & 1) == 1
    low, high = jnp.where(odd, sine, cosine), jnp.where(odd, cosine, sine)
    cos_out = jnp.where(((index + 1) & 2) == 2, -low, low)
    sin_out = jnp.where((index & 2) == 2, -high, high)
    return cos_out, sin_out


def partial_kernel(kern_hbm, traces_hbm, out_hbm, kern, rows, part, sems):
    band = lax.axis_index("band")
    get_kern = pltpu.make_async_copy(kern_hbm.at[band], kern, sems.at[0])
    get_kern.start()
    gets, puts = [], []
    for q in range(PIECES):
        at = pl.ds(q * PIECE, PIECE)
        gets.append(pltpu.make_async_copy(traces_hbm.at[at], rows.at[at], sems.at[1 + q]))
        gets[q].start()
    get_kern.wait()
    for q in range(PIECES):
        gets[q].wait()
        piece = lax.dot_general(
            kern[...],
            rows[q * PIECE : (q + 1) * PIECE],
            NT_DIMS,
            preferred_element_type=jnp.float32,
        )
        lanes = pl.ds(q * PIECE // 2, PIECE // 2)
        for b in range(BANDS):
            block = piece[b * COLS : (b + 1) * COLS]
            part[b, :, q * PIECE // 2 : (q + 1) * PIECE // 2] = jnp.concatenate(
                [block[:, : PIECE // 2], block[:, PIECE // 2 :]], axis=0
            ).astype(jnp.bfloat16)
        puts.append(
            pltpu.make_async_copy(
                part.at[:, :, lanes], out_hbm.at[:, :, lanes], sems.at[1 + PIECES + q]
            )
        )
        puts[q].start()
    for put in puts:
        put.wait()


def signed_folded(shape, dim):
    index = lax.broadcasted_iota(jnp.int32, shape, dim)
    signed = jnp.where(index < HALF, index, jnp.where(index == HALF, -HALF, HALF - index))
    return signed.astype(jnp.float32) * (2.0 * math.pi / MIDS)


def slot_kernel(
    route_hbm, x_hbm, low_ref, high_ref, offset_ref, azimuth_ref, slot_ref, bins_ref, ints, sems
):
    copies = [
        pltpu.make_async_copy(route_hbm, ints.at[0], sems.at[0]),
        pltpu.make_async_copy(x_hbm, ints.at[1], sems.at[1]),
    ]
    for copy in copies:
        copy.start()
    block = MIDS
    row_i = lax.broadcasted_iota(jnp.int32, (block, block), 0)
    col_i = lax.broadcasted_iota(jnp.int32, (block, block), 1)
    upper = jnp.where(row_i < col_i, 1.0, 0.0).astype(jnp.bfloat16)
    class_i = lax.broadcasted_iota(jnp.int32, (CLASSES * TILES, block), 0)
    for i, ref in enumerate((low_ref, high_ref, offset_ref, azimuth_ref)):
        bins_ref[i] = jnp.full((8, 128), ref[0], jnp.int32)
    for copy in copies:
        copy.wait()
    cuts = [slice(step * block, (step + 1) * block) for step in range(ROWS // block)]
    members = []
    count = jnp.zeros((CLASSES * TILES, 1), jnp.float32)
    for cut in cuts:
        kind = (ints[1, :, cut] // WIDE) * TILES + ints[0, :, cut]
        members.append(jnp.where(class_i == kind, 1.0, 0.0))
        count = count + jnp.sum(members[-1], axis=1, keepdims=True)
    none = jnp.zeros((TILES, 1), jnp.float32)
    last = CAP - 1.0
    first = jnp.concatenate(
        [none, count[:TILES], last - count[3 * TILES :], none + last], axis=0
    )
    class_row = lax.broadcasted_iota(jnp.int32, (CLASSES * TILES, 1), 0)
    step_by = jnp.where(class_row < 2 * TILES, 1.0, -1.0)
    for cut, member in zip(cuts, members):
        earlier = jnp.dot(
            member.astype(jnp.bfloat16), upper, preferred_element_type=jnp.float32
        )
        slot = jnp.sum(member * (first + step_by * earlier), axis=0, keepdims=True)
        slot_ref[:, cut] = slot.astype(jnp.int32)
        first = first + step_by * jnp.sum(member, axis=1, keepdims=True)


def phase_kernel(bins_ref, sent_hbm, phase_ref):
    first = lax.axis_index("band") * F_DEV
    low, high, offset, azimuth = (bins_ref[i, :1, :1] for i in range(4))
    h = (offset.astype(jnp.float32) + 1.0) * 0.5
    cos_t, sin_t = sincos_turns(azimuth.astype(jnp.float32) * (0.5 / AZIMUTHS))
    kx = signed_folded((MIDS, MIDS), 0)
    ky = signed_folded((MIDS, MIDS), 1)
    inline = kx * (h * cos_t) + ky * (h * sin_t)
    along = signed_folded((MIDS, 128), 0) * h
    along = jnp.log1p(along * along)
    change = jnp.concatenate([along, along], axis=1) - jnp.log1p(inline * inline)
    unit = change * (0.5 / LOG_SPAN)
    turn_c, turn_s = sincos_turns(unit)
    cos_f, sin_f = sincos_turns(unit * (first + 1).astype(jnp.float32))
    scale = ROWS**-0.5 / MIDS
    for f in range(F_DEV):
        live = (first + f >= low) & (first + f < high)
        weight = jnp.where(live, scale, 0.0)
        phase_ref[0, f] = cos_f * weight
        phase_ref[1, f] = sin_f * weight
        if f + 1 < F_DEV:
            cos_f, sin_f = cos_f * turn_c - sin_f * turn_s, cos_f * turn_s + sin_f * turn_c


def place_kernel(part_ref, rank_ref, route_ref, x_ref, y_ref, out_ref, masked):
    row = lax.broadcasted_iota(jnp.int32, (8, ROWS), 0)
    mids = jnp.where(
        row == 0,
        x_ref[...].astype(jnp.float32),
        jnp.where(row == 1, y_ref[...].astype(jnp.float32), jnp.where(row == 2, 1.0, 0.0)),
    )
    slot_i = lax.broadcasted_iota(jnp.int32, (CAP, ROWS), 0)
    slots = jnp.where(slot_i == rank_ref[...], 1.0, 0.0).astype(jnp.bfloat16)
    tile = jnp.broadcast_to(route_ref[...], (16, ROWS))
    total = part_ref[0].astype(jnp.float32)
    for b in range(1, BANDS):
        total = total + part_ref[b].astype(jnp.float32)
    total = total.astype(jnp.bfloat16).astype(jnp.float32)
    lanes = [slice(q * PIECE // 2, (q + 1) * PIECE // 2) for q in range(PIECES)]
    spectra = jnp.concatenate(
        [total[h * COLS : (h + 1) * COLS, cut] for cut in lanes for h in range(2)], axis=1
    )
    values = jnp.concatenate([spectra, mids], axis=0)
    for g in range(TILES):
        masked[g * 16 : (g + 1) * 16, :] = jnp.where(tile == g, values, 0.0).astype(jnp.bfloat16)
    placed = lax.dot_general(masked[...], slots, NT_DIMS, preferred_element_type=jnp.float32)
    out_ref[...] = placed.astype(jnp.bfloat16).reshape(TILES, 16, CAP)


def tile_kernel(
    got_ref,
    table_hbm,
    tablet_hbm,
    phase_hbm,
    out_hbm,
    xa,
    xb,
    y_all,
    parts,
    cells,
    acc,
    table,
    tablet,
    phase,
    image,
    sems,
):
    copies = [
        pltpu.make_async_copy(table_hbm, table, sems.at[0]),
        pltpu.make_async_copy(tablet_hbm, tablet, sems.at[1]),
        pltpu.make_async_copy(phase_hbm, phase, sems.at[2]),
    ]
    for copy in copies:
        copy.start()
    lane_block = lax.broadcasted_iota(jnp.int32, (16, CAP), 1) // SPAN
    for i in range(TILES // PARTS):
        held = [got_ref[i * PARTS + k].astype(jnp.float32) for k in range(PARTS)]
        for d in (1, 2, 4):
            keep = (lane_block & d) == 0
            for k in range(PARTS):
                if k & d == 0:
                    a, b = held[k], held[k + d]
                    held[k] = jnp.where(keep, a, pltpu.roll(b, SPAN * d, 1))
                    held[k + d] = jnp.where(keep, pltpu.roll(a, CAP - SPAN * d, 1), b)
        for e in range(PARTS):
            parts[e, :, i * CAP : (i + 1) * CAP] = held[e].astype(jnp.bfloat16)
    parts[PARTS] = jnp.zeros((16, DEPTH), jnp.bfloat16)
    class_i = lax.broadcasted_iota(jnp.int32, (8, DEPTH), 0)
    bit_i = lax.broadcasted_iota(jnp.int32, (8, 1), 0)
    bits = jnp.zeros((8, 1), jnp.int32)
    for e in range(PARTS):
        tail = parts[e].astype(jnp.float32)
        kind = tail[COLS : COLS + 1].astype(jnp.int32) // WIDE
        hit = jnp.where((kind == class_i) & (tail[COLS + 2 : COLS + 3] > 0.5), 1.0, 0.0)
        found = jnp.max(hit, axis=1, keepdims=True).astype(jnp.int32)
        bits = bits + lax.shift_left(found, bit_i + CLASSES * e)
    mask = jnp.sum(jnp.where(bit_i < CLASSES, bits, 0))
    number = jnp.int32(0)
    for cell in range(PARTS * CLASSES):
        cells[number] = cell
        number = number + (lax.shift_right_logical(mask, jnp.int32(cell)) & 1)
    for extra in range(FIRST + 1):
        cells[number + extra] = PARTS * CLASSES

    iota = lax.broadcasted_iota(jnp.int32, (16, CAP), 0).astype(jnp.float32)
    one = jnp.ones((16, CAP), jnp.bfloat16)
    zero = jnp.zeros((16, CAP), jnp.bfloat16)

    def build(x_buf, cell):
        part = cell // CLASSES
        start = ((cell % CLASSES) * WIDE).astype(jnp.float32)
        for i in range(DEPTH // CAP):
            cut = slice(i * CAP, (i + 1) * CAP)
            tail = parts[part, :, cut].astype(jnp.float32)
            rows = [
                jnp.broadcast_to(tail[c : c + 1], (16, CAP)).astype(jnp.bfloat16)
                for c in range(COLS + 1)
            ]
            for r in range(WIDE // 16):
                in_x = (iota + (start + 16.0 * r)).astype(jnp.bfloat16) == rows[COLS]
                for c in range(COLS):
                    at = c * WIDE + r * 16
                    x_buf[at : at + 16, cut] = jnp.where(in_x, rows[c], zero)

    def add(x_buf, cell):
        acc[cell % CLASSES] += lax.dot_general(
            x_buf[...], y_all[cell // CLASSES], NT_DIMS, preferred_element_type=jnp.float32
        )

    for e in range(PARTS):
        for i in range(DEPTH // CAP):
            cut = slice(i * CAP, (i + 1) * CAP)
            tail = parts[e, :, cut].astype(jnp.float32)
            row = jnp.broadcast_to(tail[COLS + 1 : COLS + 2], (16, CAP)).astype(jnp.bfloat16)
            for r in range(MIDS // 16):
                in_y = (iota + 16.0 * r).astype(jnp.bfloat16) == row
                y_all[e, r * 16 : (r + 1) * 16, cut] = jnp.where(in_y, one, zero)
    y_all[PARTS] = jnp.zeros((MIDS, DEPTH), jnp.bfloat16)
    acc[...] = jnp.zeros_like(acc)
    build(xa, cells[0])

    def work(first, count):
        for k in range(count):
            here, there = (xa, xb) if k % 2 == 0 else (xb, xa)
            build(there, cells[first + k + 1])
            add(here, cells[first + k])

    def more(p, _):
        work(FIRST + MORE * p, MORE)
        return 0

    def most(p, _):
        work(FIRST * p, FIRST)
        return 0

    lax.fori_loop(0, jnp.minimum(number, 1), most, 0)
    lax.fori_loop(0, (jnp.maximum(number - FIRST, 0) + MORE - 1) // MORE, more, 0)
    for copy in copies:
        copy.wait()

    lane0 = lax.broadcasted_iota(jnp.int32, (MIDS, HALF), 1) == 0
    bf = lambda v: v.astype(jnp.bfloat16)
    dot = lambda a, b: jnp.dot(a, b, preferred_element_type=jnp.float32)
    def stage_a(f):
        rows = [
            acc[q, c * WIDE : (c + 1) * WIDE]
            for c in (2 * f, 2 * f + 1)
            for q in range(CLASSES)
        ]
        u = dot(bf(jnp.concatenate(rows, axis=0)), table[...])
        cr, sr, ci, si = u[:MIDS, :HALF], u[:MIDS, HALF:], u[MIDS:, :HALF], u[MIDS:, HALF:]
        h_r = [jnp.where(lane0, cr, cr + si), jnp.where(lane0, sr, cr - si)]
        h_i = [jnp.where(lane0, ci, ci - sr), jnp.where(lane0, si, ci + sr)]
        return bf(jnp.concatenate(h_r + h_i, axis=1))

    top0 = lax.broadcasted_iota(jnp.int32, (8, MIDS), 0) == 0

    def pick_row0(zero_row, rest):
        return jnp.concatenate([jnp.where(top0, zero_row[:8], rest[:8]), rest[8:]], axis=0)

    def stage_b(f, h):
        v = dot(tablet[...], h)
        cr, sr, ci, si = v[:HALF, :MIDS], v[HALF:, :MIDS], v[:HALF, MIDS:], v[HALF:, MIDS:]
        wpr, wpi = pick_row0(cr, cr + si), pick_row0(ci, ci - sr)
        wmr, wmi = pick_row0(sr, cr - si), pick_row0(si, ci + sr)
        pc, ps = phase[0, f, :HALF], phase[1, f, :HALF]
        mc, ms = phase[0, f, HALF:], phase[1, f, HALF:]
        mpr, mpi = wpr * pc - wpi * ps, wpr * ps + wpi * pc
        mmr, mmi = wmr * mc - wmi * ms, wmr * ms + wmi * mc
        a_r, a_i = pick_row0(mpr, mpr + mmr), pick_row0(mpi, mpi + mmi)
        d_r, d_i = pick_row0(mmr, mmi - mpi), pick_row0(mmi, mpr - mmr)
        return bf(
            jnp.concatenate(
                [jnp.concatenate([a_r, a_i], axis=1), jnp.concatenate([d_r, d_i], axis=1)],
                axis=0,
            )
        )

    def stage_c(f, folded):
        q = dot(table[...], folded)
        qpr, qmr = q[:, :HALF], q[:, HALF:MIDS]
        qpi, qmi = q[:, MIDS : MIDS + HALF], q[:, MIDS + HALF :]
        a_r = jnp.where(lane0, qpr, qpr + qmr)
        a_i = jnp.where(lane0, qpi, qpi + qmi)
        d_r = jnp.where(lane0, qmr, qmi - qpi)
        d_i = jnp.where(lane0, qmi, qpr - qmr)
        return bf(
            jnp.concatenate(
                [jnp.concatenate([a_r, d_r], axis=1), jnp.concatenate([a_i, d_i], axis=1)],
                axis=0,
            )
        )

    def stage_d(f, folded):
        for i in range(2):
            cut = slice(i * MIDS, (i + 1) * MIDS)
            image[f, :, cut] = dot(folded[cut], tablet[...])
            put = pltpu.make_async_copy(
                image.at[f, :, cut], out_hbm.at[f, :, cut], sems.at[3 + 2 * f + i]
            )
            put.start()
            puts.append(put)

    puts = []
    stages = (stage_b, stage_c, stage_d)
    held = {}
    for step in range(5):
        for g in range(2):
            for f in (2 * g, 2 * g + 1):
                if g == step:
                    held[f] = stage_a(f)
                elif 0 < step - g <= 3:
                    held[f] = stages[step - g - 1](f, held[f])
    for put in puts:
        put.wait()


VM = pl.BlockSpec(memory_space=pltpu.VMEM)
SM = pl.BlockSpec(memory_space=pltpu.SMEM)
ANY = pl.BlockSpec(memory_space=pl.ANY)


def vmem(mib):
    return pltpu.CompilerParams(vmem_limit_bytes=mib * 1024 * 1024)


def cost(flops, moved):
    return pl.CostEstimate(flops=flops, bytes_accessed=moved, transcendentals=0)


def partial_spectra(kern, traces):
    return pl.pallas_call(
        partial_kernel,
        out_shape=jax.ShapeDtypeStruct((BANDS, 16, ROWS // 2), jnp.bfloat16),
        in_specs=[ANY, ANY],
        out_specs=ANY,
        scratch_shapes=[
            pltpu.VMEM((COLS * BANDS, SAMPLES), jnp.bfloat16),
            pltpu.VMEM((ROWS, SAMPLES), jnp.bfloat16),
            pltpu.VMEM((BANDS, 16, ROWS // 2), jnp.bfloat16),
            pltpu.SemaphoreType.DMA((1 + 2 * PIECES,)),
        ],
        compiler_params=vmem(60),
        cost_estimate=cost(2 * 64 * SAMPLES * ROWS, 800_000),
        name="partial_spectra",
    )(kern, traces)


def slot_ranks(route, mid_x, low, high, offset, azimuth):
    return pl.pallas_call(
        slot_kernel,
        out_shape=(
            jax.ShapeDtypeStruct((1, ROWS), jnp.int32),
            jax.ShapeDtypeStruct((4, 8, 128), jnp.int32),
        ),
        in_specs=[ANY] * 2 + [SM] * 4,
        out_specs=(VM, VM),
        scratch_shapes=[pltpu.VMEM((2, 1, ROWS), jnp.int32), pltpu.SemaphoreType.DMA((2,))],
        compiler_params=vmem(8),
        cost_estimate=cost(2_000_000_000, 3_000_000),
        name="slot_ranks",
    )(route, mid_x, low, high, offset, azimuth)


def phase_table(bins, sent):
    return pl.pallas_call(
        phase_kernel,
        out_shape=jax.ShapeDtypeStruct((2, F_DEV, MIDS, MIDS), jnp.float32),
        in_specs=[VM, ANY],
        out_specs=VM,
        compiler_params=vmem(16),
        cost_estimate=cost(2_000_000_000, 3_000_000),
        name="phase_table",
    )(bins, sent)


def place(part, rank, route, mid_x, mid_y):
    return pl.pallas_call(
        place_kernel,
        out_shape=jax.ShapeDtypeStruct((TILES, 16, CAP), jnp.bfloat16),
        in_specs=[VM] * 5,
        out_specs=VM,
        scratch_shapes=[
            pltpu.VMEM((TILES * 16, ROWS), jnp.bfloat16),
        ],
        compiler_params=vmem(16),
        cost_estimate=cost(2 * 512 * ROWS * CAP, 1_000_000),
        name="place",
    )(part, rank, route, mid_x, mid_y)


def tile_image(got, table, tablet, phase):
    return pl.pallas_call(
        tile_kernel,
        out_shape=jax.ShapeDtypeStruct((F_DEV, MIDS, 2 * MIDS), jnp.float32),
        in_specs=[VM, ANY, ANY, ANY],
        out_specs=ANY,
        scratch_shapes=[
            pltpu.VMEM((COLS * WIDE, DEPTH), jnp.bfloat16),
            pltpu.VMEM((COLS * WIDE, DEPTH), jnp.bfloat16),
            pltpu.VMEM((PARTS + 1, MIDS, DEPTH), jnp.bfloat16),
            pltpu.VMEM((PARTS + 1, 16, DEPTH), jnp.bfloat16),
            pltpu.SMEM((PARTS * CLASSES + FIRST + 2,), jnp.int32),
            pltpu.VMEM((CLASSES, COLS * WIDE, MIDS), jnp.float32),
            pltpu.VMEM((MIDS, MIDS), jnp.bfloat16),
            pltpu.VMEM((MIDS, MIDS), jnp.bfloat16),
            pltpu.VMEM((2, F_DEV, MIDS, MIDS), jnp.float32),
            pltpu.VMEM((F_DEV, MIDS, 2 * MIDS), jnp.float32),
            pltpu.SemaphoreType.DMA((3 + 2 * F_DEV,)),
        ],
        compiler_params=vmem(32),
        cost_estimate=cost(6_000_000_000, 5_000_000),
        name="tile_image",
    )(got, table, tablet, phase)


def per_device(traces, route, mid_x, mid_y, band_low, band_high, offset_bin, azimuth_bin):
    table = folded_table()
    route = route.reshape(1, ROWS)
    mid_x = mid_x.reshape(1, ROWS)
    mid_y = mid_y.reshape(1, ROWS)
    part = partial_spectra(jnp.asarray(time_kernel_blocks()), traces)
    part = lax.all_to_all(part, "band", split_axis=0, concat_axis=0, tiled=True)
    rank, bins = slot_ranks(route, mid_x, band_low, band_high, offset_bin, azimuth_bin)
    sent = place(part, rank, route, mid_x, mid_y)
    got = lax.all_to_all(sent, "tile", split_axis=0, concat_axis=0, tiled=True)
    phase = phase_table(bins, sent)
    image = tile_image(got, jnp.asarray(table), jnp.asarray(np.ascontiguousarray(table.T)), phase)
    return image[None]


def solution(mesh):
    return jax.shard_map(
        per_device,
        mesh=mesh,
        in_specs=(
            P("tile", "band"),
            P("tile", None),
            P("tile"),
            P("tile"),
            P("tile"),
            P("tile"),
            P("tile"),
            P("tile"),
        ),
        out_specs=P("tile", "band", None, None),
        check_vma=False,
    )
```

```python
import math

import jax
import jax.numpy as jnp
import numpy as np
from jax import lax
from jax.experimental import pallas as pl
from jax.experimental.pallas import tpu as pltpu
from jax.sharding import PartitionSpec as P

MIDS = 256
HALF = 128
AZIMUTHS = 12
F_DEV = 4
COLS = 2 * F_DEV
BANDS = 8
TILES = 32
ROWS = 2048
SAMPLES = 128
NT = 1024
CAP = 128
ANCHOR = 64.0
LOG_SPAN = math.log((NT + ANCHOR) / ANCHOR)
CLASSES = 4
WIDE = MIDS // CLASSES
PARTS = 8
SPAN = CAP // PARTS
DEPTH = TILES * SPAN
FIRST = 16
MORE = 4
PIECES = 1
PIECE = ROWS // PIECES
NT_DIMS = (((1,), (1,)), ((), ()))


def time_kernel_blocks():
    stretch = np.log((np.arange(NT) + ANCHOR) / ANCHOR)
    omegas = (np.arange(F_DEV * BANDS) + 1) * (2.0 * math.pi / LOG_SPAN)
    angles = omegas[:, None] * stretch[None, :]
    stacked = np.stack([np.cos(angles), -np.sin(angles)], axis=1) * NT**-0.5
    stacked = stacked.reshape(COLS * BANDS, BANDS, SAMPLES).transpose(1, 0, 2)
    return stacked.astype(np.float32).astype(jnp.bfloat16)


def folded_table():
    turns = (np.arange(MIDS)[:, None] * np.arange(HALF)[None, :]) % MIDS
    angles = turns * (2.0 * math.pi / MIDS)
    sines = np.sin(angles)
    sines[:, 0] = (-1.0) ** np.arange(MIDS)
    table = np.concatenate([np.cos(angles), sines], axis=1)
    return table.astype(np.float32).astype(jnp.bfloat16)


def sincos_turns(turns):
    quarters = (turns - jnp.round(turns)) * 4.0
    quadrant = jnp.round(quarters)
    angle = (quarters - quadrant) * (math.pi / 2)
    square = angle * angle
    sine = angle * (1.0 + square * (-1.0 / 6 + square * (1.0 / 120 + square * (-1.0 / 5040))))
    cosine = 1.0 + square * (
        -0.5 + square * (1.0 / 24 + square * (-1.0 / 720 + square * (1.0 / 40320)))
    )
    index = quadrant.astype(jnp.int32)
    odd = (index & 1) == 1
    low, high = jnp.where(odd, sine, cosine), jnp.where(odd, cosine, sine)
    cos_out = jnp.where(((index + 1) & 2) == 2, -low, low)
    sin_out = jnp.where((index & 2) == 2, -high, high)
    return cos_out, sin_out


def partial_kernel(kern_hbm, traces_hbm, out_hbm, kern, rows, part, sems):
    band = lax.axis_index("band")
    get_kern = pltpu.make_async_copy(kern_hbm.at[band], kern, sems.at[0])
    get_kern.start()
    gets, puts = [], []
    for q in range(PIECES):
        at = pl.ds(q * PIECE, PIECE)
        gets.append(pltpu.make_async_copy(traces_hbm.at[at], rows.at[at], sems.at[1 + q]))
        gets[q].start()
    get_kern.wait()
    for q in range(PIECES):
        gets[q].wait()
        piece = lax.dot_general(
            kern[...],
            rows[q * PIECE : (q + 1) * PIECE],
            NT_DIMS,
            preferred_element_type=jnp.float32,
        )
        lanes = pl.ds(q * PIECE // 2, PIECE // 2)
        for b in range(BANDS):
            block = piece[b * COLS : (b + 1) * COLS]
            part[b, :, q * PIECE // 2 : (q + 1) * PIECE // 2] = jnp.concatenate(
                [block[:, : PIECE // 2], block[:, PIECE // 2 :]], axis=0
            ).astype(jnp.bfloat16)
        puts.append(
            pltpu.make_async_copy(
                part.at[:, :, lanes], out_hbm.at[:, :, lanes], sems.at[1 + PIECES + q]
            )
        )
        puts[q].start()
    for put in puts:
        put.wait()


def signed_folded(shape, dim):
    index = lax.broadcasted_iota(jnp.int32, shape, dim)
    signed = jnp.where(index < HALF, index, jnp.where(index == HALF, -HALF, HALF - index))
    return signed.astype(jnp.float32) * (2.0 * math.pi / MIDS)


def slot_kernel(
    route_hbm, x_hbm, low_ref, high_ref, offset_ref, azimuth_ref, slot_ref, bins_ref, ints, sems
):
    copies = [
        pltpu.make_async_copy(route_hbm, ints.at[0], sems.at[0]),
        pltpu.make_async_copy(x_hbm, ints.at[1], sems.at[1]),
    ]
    for copy in copies:
        copy.start()
    block = MIDS
    row_i = lax.broadcasted_iota(jnp.int32, (block, block), 0)
    col_i = lax.broadcasted_iota(jnp.int32, (block, block), 1)
    upper = jnp.where(row_i < col_i, 1.0, 0.0).astype(jnp.bfloat16)
    class_i = lax.broadcasted_iota(jnp.int32, (CLASSES * TILES, block), 0)
    for i, ref in enumerate((low_ref, high_ref, offset_ref, azimuth_ref)):
        bins_ref[i] = jnp.full((8, 128), ref[0], jnp.int32)
    for copy in copies:
        copy.wait()
    cuts = [slice(step * block, (step + 1) * block) for step in range(ROWS // block)]
    members = []
    count = jnp.zeros((CLASSES * TILES, 1), jnp.float32)
    for cut in cuts:
        kind = (ints[1, :, cut] // WIDE) * TILES + ints[0, :, cut]
        members.append(jnp.where(class_i == kind, 1.0, 0.0))
        count = count + jnp.sum(members[-1], axis=1, keepdims=True)
    none = jnp.zeros((TILES, 1), jnp.float32)
    last = CAP - 1.0
    first = jnp.concatenate(
        [none, count[:TILES], last - count[3 * TILES :], none + last], axis=0
    )
    class_row = lax.broadcasted_iota(jnp.int32, (CLASSES * TILES, 1), 0)
    step_by = jnp.where(class_row < 2 * TILES, 1.0, -1.0)
    for cut, member in zip(cuts, members):
        earlier = jnp.dot(
            member.astype(jnp.bfloat16), upper, preferred_element_type=jnp.float32
        )
        slot = jnp.sum(member * (first + step_by * earlier), axis=0, keepdims=True)
        slot_ref[:, cut] = slot.astype(jnp.int32)
        first = first + step_by * jnp.sum(member, axis=1, keepdims=True)


def phase_kernel(bins_ref, sent_hbm, phase_ref):
    first = lax.axis_index("band") * F_DEV
    low, high, offset, azimuth = (bins_ref[i, :1, :1] for i in range(4))
    h = (offset.astype(jnp.float32) + 1.0) * 0.5
    cos_t, sin_t = sincos_turns(azimuth.astype(jnp.float32) * (0.5 / AZIMUTHS))
    kx = signed_folded((MIDS, MIDS), 0)
    ky = signed_folded((MIDS, MIDS), 1)
    inline = kx * (h * cos_t) + ky * (h * sin_t)
    along = signed_folded((MIDS, 128), 0) * h
    along = jnp.log1p(along * along)
    change = jnp.concatenate([along, along], axis=1) - jnp.log1p(inline * inline)
    unit = change * (0.5 / LOG_SPAN)
    turn_c, turn_s = sincos_turns(unit)
    cos_f, sin_f = sincos_turns(unit * (first + 1).astype(jnp.float32))
    scale = ROWS**-0.5 / MIDS
    for f in range(F_DEV):
        live = (first + f >= low) & (first + f < high)
        weight = jnp.where(live, scale, 0.0)
        phase_ref[0, f] = cos_f * weight
        phase_ref[1, f] = sin_f * weight
        if f + 1 < F_DEV:
            cos_f, sin_f = cos_f * turn_c - sin_f * turn_s, cos_f * turn_s + sin_f * turn_c


def place_kernel(
    part_ref, rank_ref, route_ref, x_ref, y_ref, out_hbm, masked, placed, sems
):
    row = lax.broadcasted_iota(jnp.int32, (8, ROWS), 0)
    mids = jnp.where(
        row == 0,
        x_ref[...].astype(jnp.float32),
        jnp.where(row == 1, y_ref[...].astype(jnp.float32), jnp.where(row == 2, 1.0, 0.0)),
    )
    slot_i = lax.broadcasted_iota(jnp.int32, (CAP, ROWS), 0)
    slots = jnp.where(slot_i == rank_ref[...], 1.0, 0.0).astype(jnp.bfloat16)
    tile = jnp.broadcast_to(route_ref[...], (16, ROWS))
    total = part_ref[0].astype(jnp.float32)
    for b in range(1, BANDS):
        total = total + part_ref[b].astype(jnp.float32)
    total = total.astype(jnp.bfloat16).astype(jnp.float32)
    lanes = [slice(q * PIECE // 2, (q + 1) * PIECE // 2) for q in range(PIECES)]
    spectra = jnp.concatenate(
        [total[h * COLS : (h + 1) * COLS, cut] for cut in lanes for h in range(2)], axis=1
    )
    values = jnp.concatenate([spectra, mids], axis=0)
    some = TILES // 2
    puts = []
    for k in range(2):
        for g in range(k * some, (k + 1) * some):
            masked[g * 16 : (g + 1) * 16, :] = jnp.where(tile == g, values, 0.0).astype(
                jnp.bfloat16
            )
        block = lax.dot_general(
            masked[k * some * 16 : (k + 1) * some * 16, :],
            slots,
            NT_DIMS,
            preferred_element_type=jnp.float32,
        )
        at = pl.ds(k * some, some)
        placed[at] = block.astype(jnp.bfloat16).reshape(some, 16, CAP)
        puts.append(pltpu.make_async_copy(placed.at[at], out_hbm.at[at], sems.at[k]))
        puts[k].start()
    for put in puts:
        put.wait()


def tile_kernel(
    got_ref,
    table_hbm,
    tablet_hbm,
    phase_hbm,
    out_hbm,
    xa,
    xb,
    y_all,
    parts,
    cells,
    acc,
    table,
    tablet,
    phase,
    image,
    sems,
):
    copies = [
        pltpu.make_async_copy(table_hbm, table, sems.at[0]),
        pltpu.make_async_copy(tablet_hbm, tablet, sems.at[1]),
        pltpu.make_async_copy(phase_hbm, phase, sems.at[2]),
    ]
    for copy in copies:
        copy.start()
    lane_block = lax.broadcasted_iota(jnp.int32, (16, CAP), 1) // SPAN
    for i in range(TILES // PARTS):
        held = [got_ref[i * PARTS + k].astype(jnp.float32) for k in range(PARTS)]
        for d in (1, 2, 4):
            keep = (lane_block & d) == 0
            for k in range(PARTS):
                if k & d == 0:
                    a, b = held[k], held[k + d]
                    held[k] = jnp.where(keep, a, pltpu.roll(b, SPAN * d, 1))
                    held[k + d] = jnp.where(keep, pltpu.roll(a, CAP - SPAN * d, 1), b)
        for e in range(PARTS):
            parts[e, :, i * CAP : (i + 1) * CAP] = held[e].astype(jnp.bfloat16)
    parts[PARTS] = jnp.zeros((16, DEPTH), jnp.bfloat16)
    class_i = lax.broadcasted_iota(jnp.int32, (8, DEPTH), 0)
    bit_i = lax.broadcasted_iota(jnp.int32, (8, 1), 0)
    bits = jnp.zeros((8, 1), jnp.int32)
    for e in range(PARTS):
        tail = parts[e].astype(jnp.float32)
        kind = tail[COLS : COLS + 1].astype(jnp.int32) // WIDE
        hit = jnp.where((kind == class_i) & (tail[COLS + 2 : COLS + 3] > 0.5), 1.0, 0.0)
        found = jnp.max(hit, axis=1, keepdims=True).astype(jnp.int32)
        bits = bits + lax.shift_left(found, bit_i + CLASSES * e)
    mask = jnp.sum(jnp.where(bit_i < CLASSES, bits, 0))
    number = jnp.int32(0)
    for cell in range(PARTS * CLASSES):
        cells[number] = cell
        number = number + (lax.shift_right_logical(mask, jnp.int32(cell)) & 1)
    for extra in range(FIRST + 1):
        cells[number + extra] = PARTS * CLASSES

    iota = lax.broadcasted_iota(jnp.int32, (16, CAP), 0).astype(jnp.float32)
    one = jnp.ones((16, CAP), jnp.bfloat16)
    zero = jnp.zeros((16, CAP), jnp.bfloat16)

    def build(x_buf, cell):
        part = cell // CLASSES
        start = ((cell % CLASSES) * WIDE).astype(jnp.float32)
        for i in range(DEPTH // CAP):
            cut = slice(i * CAP, (i + 1) * CAP)
            tail = parts[part, :, cut].astype(jnp.float32)
            rows = [
                jnp.broadcast_to(tail[c : c + 1], (16, CAP)).astype(jnp.bfloat16)
                for c in range(COLS + 1)
            ]
            for r in range(WIDE // 16):
                in_x = (iota + (start + 16.0 * r)).astype(jnp.bfloat16) == rows[COLS]
                for c in range(COLS):
                    at = c * WIDE + r * 16
                    x_buf[at : at + 16, cut] = jnp.where(in_x, rows[c], zero)

    def add(x_buf, cell):
        acc[cell % CLASSES] += lax.dot_general(
            x_buf[...], y_all[cell // CLASSES], NT_DIMS, preferred_element_type=jnp.float32
        )

    for e in range(PARTS):
        for i in range(DEPTH // CAP):
            cut = slice(i * CAP, (i + 1) * CAP)
            tail = parts[e, :, cut].astype(jnp.float32)
            row = jnp.broadcast_to(tail[COLS + 1 : COLS + 2], (16, CAP)).astype(jnp.bfloat16)
            for r in range(MIDS // 16):
                in_y = (iota + 16.0 * r).astype(jnp.bfloat16) == row
                y_all[e, r * 16 : (r + 1) * 16, cut] = jnp.where(in_y, one, zero)
    y_all[PARTS] = jnp.zeros((MIDS, DEPTH), jnp.bfloat16)
    acc[...] = jnp.zeros_like(acc)
    build(xa, cells[0])

    def work(first, count):
        for k in range(count):
            here, there = (xa, xb) if k % 2 == 0 else (xb, xa)
            build(there, cells[first + k + 1])
            add(here, cells[first + k])

    def more(p, _):
        work(FIRST + MORE * p, MORE)
        return 0

    def most(p, _):
        work(FIRST * p, FIRST)
        return 0

    lax.fori_loop(0, jnp.minimum(number, 1), most, 0)
    lax.fori_loop(0, (jnp.maximum(number - FIRST, 0) + MORE - 1) // MORE, more, 0)
    for copy in copies:
        copy.wait()

    lane0 = lax.broadcasted_iota(jnp.int32, (MIDS, HALF), 1) == 0
    bf = lambda v: v.astype(jnp.bfloat16)
    dot = lambda a, b: jnp.dot(a, b, preferred_element_type=jnp.float32)
    def stage_a(f):
        rows = [
            acc[q, c * WIDE : (c + 1) * WIDE]
            for c in (2 * f, 2 * f + 1)
            for q in range(CLASSES)
        ]
        u = dot(bf(jnp.concatenate(rows, axis=0)), table[...])
        cr, sr, ci, si = u[:MIDS, :HALF], u[:MIDS, HALF:], u[MIDS:, :HALF], u[MIDS:, HALF:]
        h_r = [jnp.where(lane0, cr, cr + si), jnp.where(lane0, sr, cr - si)]
        h_i = [jnp.where(lane0, ci, ci - sr), jnp.where(lane0, si, ci + sr)]
        return bf(jnp.concatenate(h_r + h_i, axis=1))

    top0 = lax.broadcasted_iota(jnp.int32, (8, MIDS), 0) == 0

    def pick_row0(zero_row, rest):
        return jnp.concatenate([jnp.where(top0, zero_row[:8], rest[:8]), rest[8:]], axis=0)

    def stage_b(f, h):
        v = dot(tablet[...], h)
        cr, sr, ci, si = v[:HALF, :MIDS], v[HALF:, :MIDS], v[:HALF, MIDS:], v[HALF:, MIDS:]
        wpr, wpi = pick_row0(cr, cr + si), pick_row0(ci, ci - sr)
        wmr, wmi = pick_row0(sr, cr - si), pick_row0(si, ci + sr)
        pc, ps = phase[0, f, :HALF], phase[1, f, :HALF]
        mc, ms = phase[0, f, HALF:], phase[1, f, HALF:]
        mpr, mpi = wpr * pc - wpi * ps, wpr * ps + wpi * pc
        mmr, mmi = wmr * mc - wmi * ms, wmr * ms + wmi * mc
        a_r, a_i = pick_row0(mpr, mpr + mmr), pick_row0(mpi, mpi + mmi)
        d_r, d_i = pick_row0(mmr, mmi - mpi), pick_row0(mmi, mpr - mmr)
        return bf(
            jnp.concatenate(
                [jnp.concatenate([a_r, a_i], axis=1), jnp.concatenate([d_r, d_i], axis=1)],
                axis=0,
            )
        )

    def stage_c(f, folded):
        q = dot(table[...], folded)
        qpr, qmr = q[:, :HALF], q[:, HALF:MIDS]
        qpi, qmi = q[:, MIDS : MIDS + HALF], q[:, MIDS + HALF :]
        a_r = jnp.where(lane0, qpr, qpr + qmr)
        a_i = jnp.where(lane0, qpi, qpi + qmi)
        d_r = jnp.where(lane0, qmr, qmi - qpi)
        d_i = jnp.where(lane0, qmi, qpr - qmr)
        return bf(
            jnp.concatenate(
                [jnp.concatenate([a_r, d_r], axis=1), jnp.concatenate([a_i, d_i], axis=1)],
                axis=0,
            )
        )

    def stage_d(f, folded):
        for i in range(2):
            cut = slice(i * MIDS, (i + 1) * MIDS)
            image[f, :, cut] = dot(folded[cut], tablet[...])
            put = pltpu.make_async_copy(
                image.at[f, :, cut], out_hbm.at[f, :, cut], sems.at[3 + 2 * f + i]
            )
            put.start()
            puts.append(put)

    puts = []
    stages = (stage_b, stage_c, stage_d)
    held = {}
    for step in range(5):
        for g in range(2):
            for f in (2 * g, 2 * g + 1):
                if g == step:
                    held[f] = stage_a(f)
                elif 0 < step - g <= 3:
                    held[f] = stages[step - g - 1](f, held[f])
    for put in puts:
        put.wait()


VM = pl.BlockSpec(memory_space=pltpu.VMEM)
SM = pl.BlockSpec(memory_space=pltpu.SMEM)
ANY = pl.BlockSpec(memory_space=pl.ANY)


def vmem(mib):
    return pltpu.CompilerParams(vmem_limit_bytes=mib * 1024 * 1024)


def cost(flops, moved):
    return pl.CostEstimate(flops=flops, bytes_accessed=moved, transcendentals=0)


def partial_spectra(kern, traces):
    return pl.pallas_call(
        partial_kernel,
        out_shape=jax.ShapeDtypeStruct((BANDS, 16, ROWS // 2), jnp.bfloat16),
        in_specs=[ANY, ANY],
        out_specs=ANY,
        scratch_shapes=[
            pltpu.VMEM((COLS * BANDS, SAMPLES), jnp.bfloat16),
            pltpu.VMEM((ROWS, SAMPLES), jnp.bfloat16),
            pltpu.VMEM((BANDS, 16, ROWS // 2), jnp.bfloat16),
            pltpu.SemaphoreType.DMA((1 + 2 * PIECES,)),
        ],
        compiler_params=vmem(60),
        cost_estimate=cost(2 * 64 * SAMPLES * ROWS, 800_000),
        name="partial_spectra",
    )(kern, traces)


def slot_ranks(route, mid_x, low, high, offset, azimuth):
    return pl.pallas_call(
        slot_kernel,
        out_shape=(
            jax.ShapeDtypeStruct((1, ROWS), jnp.int32),
            jax.ShapeDtypeStruct((4, 8, 128), jnp.int32),
        ),
        in_specs=[ANY] * 2 + [SM] * 4,
        out_specs=(VM, VM),
        scratch_shapes=[pltpu.VMEM((2, 1, ROWS), jnp.int32), pltpu.SemaphoreType.DMA((2,))],
        compiler_params=vmem(8),
        cost_estimate=cost(2_000_000_000, 3_000_000),
        name="slot_ranks",
    )(route, mid_x, low, high, offset, azimuth)


def phase_table(bins, sent):
    return pl.pallas_call(
        phase_kernel,
        out_shape=jax.ShapeDtypeStruct((2, F_DEV, MIDS, MIDS), jnp.float32),
        in_specs=[VM, ANY],
        out_specs=VM,
        compiler_params=vmem(16),
        cost_estimate=cost(2_000_000_000, 3_000_000),
        name="phase_table",
    )(bins, sent)


def place(part, rank, route, mid_x, mid_y):
    return pl.pallas_call(
        place_kernel,
        out_shape=jax.ShapeDtypeStruct((TILES, 16, CAP), jnp.bfloat16),
        in_specs=[VM] * 5,
        out_specs=ANY,
        scratch_shapes=[
            pltpu.VMEM((TILES * 16, ROWS), jnp.bfloat16),
            pltpu.VMEM((TILES, 16, CAP), jnp.bfloat16),
            pltpu.SemaphoreType.DMA((2,)),
        ],
        compiler_params=vmem(16),
        cost_estimate=cost(2 * 512 * ROWS * CAP, 1_000_000),
        name="place",
    )(part, rank, route, mid_x, mid_y)


def tile_image(got, table, tablet, phase):
    return pl.pallas_call(
        tile_kernel,
        out_shape=jax.ShapeDtypeStruct((F_DEV, MIDS, 2 * MIDS), jnp.float32),
        in_specs=[VM, ANY, ANY, ANY],
        out_specs=ANY,
        scratch_shapes=[
            pltpu.VMEM((COLS * WIDE, DEPTH), jnp.bfloat16),
            pltpu.VMEM((COLS * WIDE, DEPTH), jnp.bfloat16),
            pltpu.VMEM((PARTS + 1, MIDS, DEPTH), jnp.bfloat16),
            pltpu.VMEM((PARTS + 1, 16, DEPTH), jnp.bfloat16),
            pltpu.SMEM((PARTS * CLASSES + FIRST + 2,), jnp.int32),
            pltpu.VMEM((CLASSES, COLS * WIDE, MIDS), jnp.float32),
            pltpu.VMEM((MIDS, MIDS), jnp.bfloat16),
            pltpu.VMEM((MIDS, MIDS), jnp.bfloat16),
            pltpu.VMEM((2, F_DEV, MIDS, MIDS), jnp.float32),
            pltpu.VMEM((F_DEV, MIDS, 2 * MIDS), jnp.float32),
            pltpu.SemaphoreType.DMA((3 + 2 * F_DEV,)),
        ],
        compiler_params=vmem(32),
        cost_estimate=cost(6_000_000_000, 5_000_000),
        name="tile_image",
    )(got, table, tablet, phase)


def per_device(traces, route, mid_x, mid_y, band_low, band_high, offset_bin, azimuth_bin):
    table = folded_table()
    route = route.reshape(1, ROWS)
    mid_x = mid_x.reshape(1, ROWS)
    mid_y = mid_y.reshape(1, ROWS)
    part = partial_spectra(jnp.asarray(time_kernel_blocks()), traces)
    part = lax.all_to_all(part, "band", split_axis=0, concat_axis=0, tiled=True)
    rank, bins = slot_ranks(route, mid_x, band_low, band_high, offset_bin, azimuth_bin)
    sent = place(part, rank, route, mid_x, mid_y)
    got = lax.all_to_all(sent, "tile", split_axis=0, concat_axis=0, tiled=True)
    phase = phase_table(bins, sent)
    image = tile_image(got, jnp.asarray(table), jnp.asarray(np.ascontiguousarray(table.T)), phase)
    return image[None]


def solution(mesh):
    return jax.shard_map(
        per_device,
        mesh=mesh,
        in_specs=(
            P("tile", "band"),
            P("tile", None),
            P("tile"),
            P("tile"),
            P("tile"),
            P("tile"),
            P("tile"),
            P("tile"),
        ),
        out_specs=P("tile", "band", None, None),
        check_vma=False,
    )
```
